32 devices in a mesh: pair: 4 (over y, x), tensor: 8 (over z, core).
Axes of the slice: x: 2, y: 2, z: 4, core: 2. Of those that a mesh axis runs over, the one named last changes fastest.
Arguments:
- queries: bfloat16 [8, 64, 1024], P('pair', 'tensor'), may hold values from -6 to 6
- documents: bfloat16 [16, 128, 1024], P('pair', 'tensor'), may hold values from -6 to 6
- doc_len: int32 [16], replicated, may hold values from 32 to 128
- route: int32 [4, 4], replicated, may hold values from -1 to 3, as said below
- pair_list: int32 [12, 3], P('pair'), may hold values from 0 to 3, as said below
- attn_gain: float32 [1024], replicated
- w_query: bfloat16 [1024, 8192], P(None, 'tensor')
- w_key: bfloat16 [1024, 8192], P(None, 'tensor')
- w_value: bfloat16 [1024, 8192], P(None, 'tensor'), may hold values from -0.1875 to 0.1875
- w_output: bfloat16 [8192, 1024], P('tensor'), may hold values from -0.5 to 0.5
- ffn_gain: float32 [1024], replicated, may hold values from 0.1 to 1.9
- w_in: bfloat16 [1024, 32768], P(None, 'tensor'), may hold values from -0.1875 to 0.1875
- w_down: bfloat16 [32768, 1024], P('tensor'), may hold values from -0.25 to 0.25
Outputs:
- doc_states: bfloat16 [16, 128, 1024], P('pair', 'tensor')
The draws below stay inside these ranges and needn't reach their ends.
Inputs may be any that keep to these rules, and one draw needn't show every extreme that they name: route[s, g] is the local index, among the 4 documents of pair index s, of the one document s sends to owner g, or -1 where it sends none; each owner receives exactly min(6, number of pair indices) documents. `pair_list`: rows p * 3 to p * 3 + 2 belong to owner p; column 0 is below 2; columns 1 and 2 differ and name pair indices that send a document to that owner; each document an owner receives fills one or more roles of its pairs.
All inputs are finite; a program needn't handle non-finite values.
Results may differ from the reference program's by a relative error of at most 0.018.
Values may be sent and summed in bfloat16 or wider, within the bound.
No kernel may reach another device: no remote copies, remote signals or barrier semaphores. Data moves between devices by JAX's collectives and lax.ppermute only.
A program may use at most 128 MiB of HBM per device.

```python
import jax
import jax.numpy as jnp
from jax import lax

D = 1024
HEAD = 128
HEADS = 64
FF = 32768
QLEN = 64
DLEN = 128
QUERY_DEV = 2
PAIRS_DEV = 3
DOC_DEV = 4
ROW = 320
NPAIRS = 12
NDOC = 16
NQUERY = 8


def pair_tables(key):
    owners_count = NDOC // DOC_DEV
    needed = min(2 * PAIRS_DEV, owners_count)
    orders = jax.vmap(lambda owner: jax.random.permutation(jax.random.fold_in(key, owner), owners_count))(jnp.arange(owners_count, dtype=jnp.int32))
    sources = orders[:, :needed].astype(jnp.int32)
    picked = jax.random.randint(jax.random.fold_in(key, 1001), (owners_count, needed), 0, DOC_DEV, dtype=jnp.int32)
    targets = jnp.broadcast_to(jnp.arange(owners_count, dtype=jnp.int32)[:, None], (owners_count, needed))
    table = jnp.full((owners_count, owners_count), -1, jnp.int32)
    table = table.at[sources, targets].set(picked)
    role_index = jnp.arange(2 * PAIRS_DEV, dtype=jnp.int32) % needed
    role_sources = sources[:, role_index]
    chosen = jax.random.randint(jax.random.fold_in(key, 1002), (owners_count, PAIRS_DEV), 0, QUERY_DEV, dtype=jnp.int32)
    listing = jnp.stack([chosen, role_sources[:, 0::2], role_sources[:, 1::2]], -1).reshape(owners_count * PAIRS_DEV, 3)
    return (table, listing.astype(jnp.int32))


def draw_route(key, part):
    return pair_tables(jax.random.fold_in(key, 77))[0]


def draw_pair_list(key, part):
    return pair_tables(jax.random.fold_in(key, 77))[1]


def projection_pair(key):
    shape = (D, HEADS * HEAD)
    base = jax.random.normal(jax.random.fold_in(key, 5), shape, jnp.float32) / jnp.sqrt(jnp.float32(D))
    noise = jax.random.normal(jax.random.fold_in(key, 6), shape, jnp.float32) / jnp.sqrt(jnp.float32(D))
    second = noise
    return (base.astype(jnp.bfloat16), second.astype(jnp.bfloat16))


def draw_w_query(key, part):
    return projection_pair(jax.random.fold_in(key, 91))[0]


def draw_w_key(key, part):
    return projection_pair(jax.random.fold_in(key, 91))[1]


def draw_attn_gain(key, part):
    return jax.random.uniform(jax.random.fold_in(key, 3), (D,), jnp.float32, 0.6, 1.4)


def touch_ends(drawn, stream_key, least, largest):
    place = [jax.random.randint(jax.random.fold_in(stream_key, axis), (), 0, length) for axis, length in enumerate(drawn.shape)]
    longest = drawn.shape.index(max(drawn.shape))
    beside = place[:longest] + [(place[longest] + 1) % drawn.shape[longest]] + place[longest + 1:]
    return drawn.at[tuple(place)].set(least).at[tuple(beside)].set(largest)


def block_levels(stream_key, extent, split, low, high):
    def one(axis_at, blocks):
        steps = jax.random.uniform(jax.random.fold_in(jax.random.fold_in(stream_key, 6), axis_at), (blocks,), jnp.float32, low / len(split), high / len(split))
        return jnp.repeat(jnp.exp(steps), extent[axis_at] // blocks).reshape((-1,) + (1,) * (len(extent) - axis_at - 1))

    level = one(*split[0])
    for cut in split[1:]:
        level = level * one(*cut)
    return level


def normal_values(key, shape, width, reach, cuts=(), kind=jnp.bfloat16):
    level = block_levels(key, shape, cuts, -0.22, 0.18) if cuts else 1.0
    values = jax.random.normal(key, shape, jnp.float32) * width * level
    return jnp.minimum(jnp.maximum(values, -reach), reach).astype(kind)


def setup_inputs(seed: int = 0) -> dict:
    arg_keys = jax.random.split(jax.random.key(seed), 14)
    return {
        "queries": normal_values(arg_keys[0], (NQUERY, QLEN, D), 1.0, 6.0, ((0, 4), (1, 8))),
        "documents": normal_values(arg_keys[1], (NDOC, DLEN, D), 1.0, 6.0, ((0, 4), (1, 8))),
        "doc_len": touch_ends(jax.random.randint(arg_keys[2], (NDOC,), DLEN // 4, DLEN + 1), jax.random.fold_in(arg_keys[2], 1), DLEN // 4, DLEN).astype(jnp.int32),
        "route": draw_route(jax.random.fold_in(arg_keys[13], 71), 0),
        "pair_list": draw_pair_list(jax.random.fold_in(arg_keys[13], 71), 0),
        "attn_gain": draw_attn_gain(jax.random.fold_in(arg_keys[13], 71), 0),
        "w_query": draw_w_query(jax.random.fold_in(arg_keys[13], 71), 0),
        "w_key": draw_w_key(jax.random.fold_in(arg_keys[13], 71), 0),
        "w_value": normal_values(arg_keys[8], (D, HEADS * HEAD), D ** -0.5, 0.1875, ((1, 8),)),
        "w_output": normal_values(arg_keys[9], (HEADS * HEAD, D), (HEADS * HEAD // 64) ** -0.5, 0.5, ((0, 8),)),
        "ffn_gain": jnp.clip(1.0 + 0.18 * jax.random.normal(arg_keys[10], (D,), jnp.float32), 0.1, 1.9),
        "w_in": normal_values(arg_keys[11], (D, FF), D ** -0.5, 0.1875, ((1, 8),)),
        "w_down": normal_values(arg_keys[12], (FF, D), (FF // 64) ** -0.5, 0.25, ((0, 8),)),
    }


def rms_norm(values, gain):
    spread = lax.optimization_barrier(jnp.mean(values * values, -1, keepdims=True))
    return values * lax.rsqrt(spread + 1e-06) * gain

def reference(queries, documents, doc_len, route, pair_list, attn_gain, w_query, w_key, w_value, w_output, ffn_gain, w_in, w_down):
    owners = jnp.arange(NPAIRS, dtype=jnp.int32) // PAIRS_DEV
    first_src = pair_list[:, 1].astype(jnp.int32)
    second_src = pair_list[:, 2].astype(jnp.int32)
    first_ids = (first_src * DOC_DEV + route[first_src, owners]).astype(jnp.int32)
    second_ids = (second_src * DOC_DEV + route[second_src, owners]).astype(jnp.int32)
    query_ids = (owners * QUERY_DEV + pair_list[:, 0]).astype(jnp.int32)

    def pair_states(items):
        query_id, first_doc, second_doc = items
        row_tokens = jnp.concatenate([queries[query_id], documents[first_doc], documents[second_doc]], 0)
        position = jnp.arange(ROW, dtype=jnp.int32)
        first_ok = (position >= QLEN) & (position < QLEN + DLEN) & (position - QLEN < doc_len[first_doc])
        second_ok = (position >= QLEN + DLEN) & (position - QLEN - DLEN < doc_len[second_doc])
        key_ok = (position < QLEN) | first_ok | second_ok
        values = row_tokens.astype(jnp.float32)
        normed = rms_norm(values, attn_gain).astype(jnp.bfloat16)
        query_heads = jnp.dot(normed, w_query, preferred_element_type=jnp.float32).astype(jnp.bfloat16).reshape(ROW, HEADS, HEAD)
        key_heads = jnp.dot(normed, w_key, preferred_element_type=jnp.float32).astype(jnp.bfloat16).reshape(ROW, HEADS, HEAD)
        value_heads = jnp.dot(normed, w_value, preferred_element_type=jnp.float32).astype(jnp.bfloat16).reshape(ROW, HEADS, HEAD)
        scores = jnp.einsum('rhd,shd->hrs', query_heads.astype(jnp.float32), key_heads.astype(jnp.float32), precision=lax.Precision.HIGHEST) / jnp.sqrt(jnp.float32(HEAD))
        scores = jnp.where(key_ok[None, None, :], scores, jnp.float32(-1e+30))
        top = lax.optimization_barrier(jnp.max(scores, -1, keepdims=True))
        expo = jnp.exp(scores - top)
        probs = (expo / lax.optimization_barrier(jnp.sum(expo, -1, keepdims=True))).astype(jnp.bfloat16)
        context = jnp.einsum('hrs,shd->rhd', probs.astype(jnp.float32), value_heads.astype(jnp.float32), precision=lax.Precision.HIGHEST)
        context = context.astype(jnp.bfloat16).reshape(ROW, HEADS * HEAD)
        hidden_state = values + jnp.dot(context, w_output, preferred_element_type=jnp.float32)
        ffn_in = rms_norm(hidden_state, ffn_gain).astype(jnp.bfloat16)
        units = jax.nn.relu(jnp.dot(ffn_in, w_in, preferred_element_type=jnp.float32)).astype(jnp.bfloat16)
        layer_out = hidden_state + jnp.dot(units, w_down, preferred_element_type=jnp.float32)
        first_seg = layer_out[QLEN:QLEN + DLEN] * first_ok[QLEN:QLEN + DLEN, None].astype(jnp.float32)
        second_seg = layer_out[QLEN + DLEN:] * second_ok[QLEN + DLEN:, None].astype(jnp.float32)
        return (first_seg, second_seg)
    first_all, second_all = lax.map(pair_states, (query_ids, first_ids, second_ids))
    doc_range = jnp.arange(NDOC, dtype=jnp.int32)
    first_pick = (first_ids[:, None] == doc_range[None, :]).astype(jnp.float32)
    second_pick = (second_ids[:, None] == doc_range[None, :]).astype(jnp.float32)
    totals = jnp.einsum('pn,pld->nld', first_pick, first_all, precision=lax.Precision.HIGHEST)
    totals = totals + jnp.einsum('pn,pld->nld', second_pick, second_all, precision=lax.Precision.HIGHEST)
    return totals.astype(jnp.bfloat16)
```

```python
import functools
import math

import jax
import jax.numpy as jnp
from jax import lax
from jax.experimental import pallas as pl
from jax.experimental.pallas import tpu as pltpu
from jax.sharding import PartitionSpec as P

HEAD = 128
LIMIT = 32 * 1024 * 1024


def rms_norm(values, gain):
    spread = jnp.mean(values * values, -1, keepdims=True)
    return values * lax.rsqrt(spread + 1e-06) * gain


def swap(values, bit, axis):
    count = lax.axis_size(axis)
    return lax.ppermute(values, axis, [(i, i ^ bit) for i in range(count)])


def gather_blocks(values, bits):
    for bit in bits:
        values = jnp.concatenate([values, swap(values, bit, "tensor")], 1)
    return values


def halve(values, bit):
    half = values.shape[1] // 2
    return values[:, :half], swap(values[:, half:], bit, "tensor")


def attend_kernel(pair, bits, meta, q_ref, kd_ref, vd_ref, kq_ref, vq_ref, wo_ref, out_ref, ctx_ref):
    slots, blocks, rows, width = q_ref.shape
    keys = blocks * rows
    my_slice = meta[0, 5]
    query, first, second = meta[pair, 0], meta[pair, 1], meta[pair, 2]
    lane = lax.broadcasted_iota(jnp.int32, (1, keys), 1)
    block, row = lane // rows, lane % rows
    origin = jnp.zeros_like(lane)
    for place, bit in enumerate(bits):
        origin = origin + ((block >> place) & 1) * bit
    position = (origin ^ my_slice) * rows + row
    low = jnp.float32(-1e30)
    bias_first = jnp.where(position < meta[pair, 3], 0.0, low)
    bias_second = jnp.where(position < meta[pair, 4], 0.0, low)
    query_keys = kq_ref.shape[1] * kq_ref.shape[2]
    bias = jnp.concatenate([bias_first, bias_second, jnp.zeros((1, query_keys), jnp.float32)], 1)
    scale = math.log2(math.e) / math.sqrt(HEAD)

    def both(ref, at):
        return [ref[first, :, :, at].reshape(keys, HEAD), ref[second, :, :, at].reshape(keys, HEAD)]

    for head in range(width // HEAD):
        at = slice(head * HEAD, (head + 1) * HEAD)
        qs = jnp.concatenate(both(q_ref, at), 0)
        ks = jnp.concatenate(both(kd_ref, at) + [kq_ref[query, :, :, at].reshape(query_keys, HEAD)], 0)
        vs = jnp.concatenate(both(vd_ref, at) + [vq_ref[query, :, :, at].reshape(query_keys, HEAD)], 0)
        scores = lax.dot_general(qs, ks, (((1,), (1,)), ((), ())), preferred_element_type=jnp.float32)
        scores = scores * scale + bias
        top = jnp.max(scores, -1, keepdims=True)
        expo = jnp.exp2(scores - top)
        total = jnp.sum(expo, -1, keepdims=True)
        mixed = jnp.dot(expo.astype(jnp.bfloat16), vs, preferred_element_type=jnp.float32)
        ctx_ref[:, at] = (mixed / total).astype(jnp.bfloat16)
    product = jnp.dot(ctx_ref[...], wo_ref[...], preferred_element_type=jnp.float32)
    out_ref[...] = product.astype(jnp.bfloat16).reshape(out_ref.shape)


def attend(pair, bits, meta, q, kd, vd, kq, vq, w_output):
    slots, blocks, rows, width = q.shape
    model = w_output.shape[1]
    full = lambda a: pl.BlockSpec(a.shape, lambda i, m, n=a.ndim: (0,) * n)
    ops = (q, kd, vd, kq, vq, w_output)
    return pl.pallas_call(
        functools.partial(attend_kernel, pair, bits),
        out_shape=jax.ShapeDtypeStruct((2, blocks, rows, model), jnp.bfloat16),
        grid_spec=pltpu.PrefetchScalarGridSpec(
            num_scalar_prefetch=1,
            grid=(1,),
            in_specs=[full(a) for a in ops],
            out_specs=pl.BlockSpec((2, blocks, rows, model), lambda i, m: (0, 0, 0, 0)),
            scratch_shapes=[pltpu.VMEM((2 * blocks * rows, width), jnp.bfloat16)],
        ),
        compiler_params=pltpu.CompilerParams(vmem_limit_bytes=LIMIT),
        cost_estimate=pl.CostEstimate(
            flops=2 * 2 * blocks * rows * width * (model + 6 * blocks * rows),
            bytes_accessed=2 * model * width,
            transcendentals=width // HEAD * 6 * (blocks * rows) ** 2,
        ),
        name="attend",
    )(meta, *ops)


def settle_kernel(pair, meta, kept_ref, came_ref, rows_ref, gain_ref, hidden_ref, ffn_ref):
    for role in range(2):
        slot = meta[pair, 1 + role]
        summed = kept_ref[role, 0].astype(jnp.float32) + came_ref[role, 0].astype(jnp.float32)
        summed = summed.astype(jnp.bfloat16).astype(jnp.float32)
        hidden = rows_ref[slot].astype(jnp.float32) + summed
        hidden_ref[role] = hidden
        ffn_ref[role, 0] = rms_norm(hidden, gain_ref[...]).astype(jnp.bfloat16)


def settle(pair, meta, kept, came, rows, gain):
    _, _, count, width = kept.shape
    full = lambda a: pl.BlockSpec(a.shape, lambda i, m, n=a.ndim: (0,) * n)
    ops = (kept, came, rows, gain.reshape(1, width))
    return pl.pallas_call(
        functools.partial(settle_kernel, pair),
        out_shape=[
            jax.ShapeDtypeStruct((2, count, width), jnp.float32),
            jax.ShapeDtypeStruct((2, 1, count, width), jnp.bfloat16),
        ],
        grid_spec=pltpu.PrefetchScalarGridSpec(
            num_scalar_prefetch=1,
            grid=(1,),
            in_specs=[full(a) for a in ops],
            out_specs=[
                pl.BlockSpec((2, count, width), lambda i, m: (0, 0, 0)),
                pl.BlockSpec((2, 1, count, width), lambda i, m: (0, 0, 0, 0)),
            ],
        ),
        compiler_params=pltpu.CompilerParams(vmem_limit_bytes=LIMIT),
        name="settle",
    )(meta, *ops)


def expand_kernel(pair, first_call, meta, kept_ref, came_ref, w_ref, *rest):
    old_ref, out_ref = (None, rest[0]) if first_call else rest
    _, half, rows, width = kept_ref.shape
    tall = 2 * half * rows
    tile = w_ref.shape[1]
    tokens = jnp.concatenate(
        [kept_ref[...].reshape(tall, width), came_ref[...].reshape(tall, width)], 0
    )
    units = jnp.maximum(jnp.dot(tokens, w_ref[...], preferred_element_type=jnp.float32), 0.0)
    out_ref[...] = jnp.zeros_like(out_ref) if first_call else old_ref[...]
    for role in range(2):
        slot = meta[pair, 1 + role]
        for part in range(2):
            begin = part * tall + role * half * rows
            new = units[begin : begin + half * rows].reshape(half, rows, tile)
            here = pl.ds(part * half, half)
            held = out_ref[slot, here].astype(jnp.float32)
            out_ref[slot, here] = (held + new.astype(jnp.bfloat16).astype(jnp.float32)).astype(jnp.bfloat16)


def expand(pair, meta, kept, came, w_in, slots, old):
    _, half, rows, width = kept.shape
    units = w_in.shape[1]
    tile = min(1024, units)
    full = lambda a: pl.BlockSpec(a.shape, lambda i, m, n=a.ndim: (0,) * n)
    held = pl.BlockSpec((slots, 2 * half, rows, tile), lambda i, m: (0, 0, 0, i))
    ops = (kept, came, w_in) + (() if old is None else (old,))
    specs = [full(kept), full(came), pl.BlockSpec((width, tile), lambda i, m: (0, i))]
    return pl.pallas_call(
        functools.partial(expand_kernel, pair, old is None),
        out_shape=jax.ShapeDtypeStruct((slots, 2 * half, rows, units), jnp.bfloat16),
        grid_spec=pltpu.PrefetchScalarGridSpec(
            num_scalar_prefetch=1,
            grid=(units // tile,),
            in_specs=specs + ([] if old is None else [held]),
            out_specs=held,
        ),
        input_output_aliases={} if old is None else {4: 0},
        compiler_params=pltpu.CompilerParams(vmem_limit_bytes=LIMIT),
        cost_estimate=pl.CostEstimate(
            flops=2 * 4 * half * rows * width * units,
            bytes_accessed=2 * width * units,
            transcendentals=0,
        ),
        name="expand",
    )(meta, *ops)


def local(
    queries,
    documents,
    doc_len,
    route,
    pair_list,
    attn_gain,
    w_query,
    w_key,
    w_value,
    w_output,
    ffn_gain,
    w_in,
    w_down,
):
    owners = lax.axis_size("pair")
    slices = lax.axis_size("tensor")
    me = lax.axis_index("pair")
    my_slice = lax.axis_index("tensor")
    doc_count, doc_rows, width = documents.shape
    query_count, query_rows, _ = queries.shape
    pairs = pair_list.shape[0]
    slots = min(2 * pairs, owners)
    heads_width = w_query.shape[1]
    down_bits = [1 << i for i in range(slices.bit_length() - 1)]
    up_bits = down_bits[::-1]

    partner = me ^ jnp.arange(owners, dtype=jnp.int32)
    sent = jnp.maximum(lax.dynamic_slice_in_dim(route, me, 1, 0)[0], 0)
    incoming = lax.dynamic_slice_in_dim(route, me, 1, 1)[:, 0]
    source_len = jnp.sum(
        jnp.where(
            (jnp.arange(owners, dtype=jnp.int32) * doc_count + incoming)[:, None]
            == jnp.arange(doc_len.shape[0], dtype=jnp.int32)[None, :],
            doc_len[None, :],
            0,
        ),
        1,
    )
    taken = (incoming >= 0).astype(jnp.int32)
    if slots == owners:
        slot_of_source = partner
    else:
        earlier = jnp.arange(owners)[:, None] > jnp.arange(owners)[None, :]
        slot_of_source = jnp.sum(jnp.where(earlier, taken[None, :], 0), 1)

    def pick(table, index):
        return jnp.sum(jnp.where(jnp.arange(owners, dtype=jnp.int32) == index, table, 0))

    def by_source(table, index):
        return jnp.sum(
            jnp.where(index[:, None] == jnp.arange(owners, dtype=jnp.int32)[None, :], table[None, :], 0), 1
        )

    first, second = pair_list[:, 1], pair_list[:, 2]
    meta = jnp.stack(
        [
            pair_list[:, 0],
            by_source(slot_of_source, first),
            by_source(slot_of_source, second),
            by_source(source_len, first),
            by_source(source_len, second),
            jnp.full((pairs,), my_slice, jnp.int32),
        ],
        1,
    )

    arrived = []
    for k in range(owners):
        block = lax.dynamic_index_in_dim(documents, pick(sent, partner[k]), 0, False)
        arrived.append(block if k == 0 else swap(block, k, "pair"))
    norm = lambda a: rms_norm(a.astype(jnp.float32), attn_gain).astype(jnp.bfloat16)
    own_queries = norm(queries).reshape(1, 1, query_count * query_rows, width)
    if slots == owners:
        rows_own = jnp.stack(arrived)
        early = jnp.concatenate([norm(arrived[0])[None, None], own_queries], 2)
        late = norm(jnp.stack(arrived[1:]))[:, None]
    else:
        place = jnp.stack([jnp.where(pick(taken, partner[k]) > 0, pick(slot_of_source, partner[k]), -1) for k in range(owners)])
        rows_own = jnp.einsum(
            "sk,krd->srd",
            (jnp.arange(slots, dtype=jnp.int32)[:, None] == place[None, :]).astype(jnp.bfloat16),
            jnp.stack(arrived),
            preferred_element_type=jnp.float32,
        ).astype(jnp.bfloat16)
        early = own_queries
        late = norm(rows_own)[:, None]

    early = gather_blocks(early, up_bits)
    late = gather_blocks(late, up_bits)

    def project(rows, w):
        return jnp.einsum("sbrd,de->sbre", rows, w, preferred_element_type=jnp.float32).astype(jnp.bfloat16)

    early_docs = early.shape[2] - query_count * query_rows
    split_queries = lambda a: a[0, :, early_docs:].reshape(slices, query_count, query_rows, heads_width).swapaxes(0, 1)
    early_k, early_v = project(early, w_key), project(early, w_value)
    kq, vq = split_queries(early_k), split_queries(early_v)
    q, kd, vd = project(late, w_query), project(late, w_key), project(late, w_value)
    if early_docs:
        q = jnp.concatenate([project(early[:, :, :early_docs], w_query), q], 0)
        kd = jnp.concatenate([early_k[:, :, :early_docs], kd], 0)
        vd = jnp.concatenate([early_v[:, :, :early_docs], vd], 0)

    hidden, units = [], None
    for pair in range(pairs):
        part = attend(pair, up_bits, meta, q, kd, vd, kq, vq, w_output)
        for bit in down_bits:
            kept, came = halve(part, bit)
            if bit != down_bits[-1]:
                part = kept + came
        own, ffn = settle(pair, meta, kept, came, rows_own, ffn_gain)
        hidden.append(own)
        ffn = gather_blocks(ffn, up_bits[:-1])
        other = swap(ffn, up_bits[-1], "tensor")
        units = expand(pair, meta, ffn, other, w_in, slots, units)

    parts = []
    columns = 2
    step = width // columns
    for c in range(columns):
        part = jnp.einsum(
            "sbrf,fd->sbrd", units, w_down[:, c * step : (c + 1) * step], preferred_element_type=jnp.float32
        ).astype(jnp.bfloat16)
        for bit in down_bits:
            kept, came = halve(part, bit)
            part = kept + came
        parts.append(part[:, 0])
    total = jnp.concatenate(parts, 2).astype(jnp.float32)
    hidden = jnp.stack(hidden)
    picks = meta[:, 1:3, None] == jnp.arange(slots, dtype=jnp.int32)[None, None, :]
    slot_len = jnp.max(jnp.where(picks, meta[:, 3:5, None], 0), (0, 1))
    for p in range(pairs):
        for role in range(2):
            total = total + jnp.where(picks[p, role][:, None, None], hidden[p, role][None], 0.0)
    position = my_slice * doc_rows + jnp.arange(doc_rows, dtype=jnp.int32)
    total = jnp.where((position[None, :] < slot_len[:, None])[:, :, None], total, 0.0).astype(jnp.bfloat16)

    result = jnp.zeros((doc_count, doc_rows, width), jnp.float32)
    outgoing = lax.dynamic_slice_in_dim(route, me, 1, 0)[0]
    for k in range(owners):
        if slots == owners:
            block = total[k]
        else:
            here = (jnp.arange(slots, dtype=jnp.int32) == place[k])[:, None, None]
            block = jnp.sum(jnp.where(here, total.astype(jnp.float32), 0.0), 0).astype(jnp.bfloat16)
        if k:
            block = swap(block, k, "pair")
        target = pick(outgoing, partner[k])
        here = (target == jnp.arange(doc_count, dtype=jnp.int32))[:, None, None]
        result = result + jnp.where(here, block.astype(jnp.float32)[None], 0.0)
    return result.astype(jnp.bfloat16)


def solution(mesh):
    placed = (
        P("pair", "tensor", None),
        P("pair", "tensor", None),
        P(),
        P(),
        P("pair", None),
        P(),
        P(None, "tensor"),
        P(None, "tensor"),
        P(None, "tensor"),
        P("tensor", None),
        P(),
        P(None, "tensor"),
        P("tensor", None),
    )
    return jax.shard_map(
        local, mesh=mesh, in_specs=placed, out_specs=P("pair", "tensor", None), check_vma=False
    )
```

```python
import functools
import math

import jax
import jax.numpy as jnp
from jax import lax
from jax.experimental import pallas as pl
from jax.experimental.pallas import tpu as pltpu
from jax.sharding import PartitionSpec as P

HEAD = 128
MIB = 1024 * 1024


def rms_norm(values, gain):
    spread = jnp.mean(values * values, -1, keepdims=True)
    return values * lax.rsqrt(spread + 1e-06) * gain


def swap(values, bit, axis):
    count = lax.axis_size(axis)
    return lax.ppermute(values, axis, [(i, i ^ bit) for i in range(count)])


def gather_blocks(values, bits):
    for bit in bits:
        values = jnp.concatenate([values, swap(values, bit, "tensor")], 1)
    return values


def halve(values, bit):
    half = values.shape[1] // 2
    return values[:, :half], swap(values[:, half:], bit, "tensor")


def kernel_call(kernel, name, operands, out_shape, scratch=(), smem=(), out_smem=(), limit=16, flops=0, moved=0, exps=0):
    space = lambda yes: pl.BlockSpec(memory_space=pltpu.SMEM if yes else pltpu.VMEM)
    return pl.pallas_call(
        kernel,
        out_shape=out_shape,
        in_specs=[space(i in smem) for i in range(len(operands))],
        out_specs=[space(i in out_smem) for i in range(len(out_shape))],
        scratch_shapes=list(scratch),
        compiler_params=pltpu.CompilerParams(vmem_limit_bytes=limit * MIB),
        cost_estimate=pl.CostEstimate(flops=flops, bytes_accessed=moved, transcendentals=exps),
        name=name,
    )(*operands)


def bf16(*shape):
    return jax.ShapeDtypeStruct(shape, jnp.bfloat16)


def start_kernel(slots, route_ref, len_ref, list_ref, docs_ref, queries_ref, gain_ref, meta_ref, early_ref, *send_refs):
    owners = route_ref.shape[0]
    doc_count, doc_rows, width = docs_ref.shape
    me = lax.axis_index("pair")
    for k in range(owners):
        picked = docs_ref[jnp.maximum(route_ref[me, me ^ k], 0)]
        send_refs[k][...] = picked
        if k == 0 and slots == owners:
            own = picked.astype(jnp.float32)
            early_ref[1, 0] = rms_norm(own, gain_ref[...]).astype(jnp.bfloat16)
    tokens = queries_ref[...].astype(jnp.float32).reshape(early_ref.shape[2], width)
    early_ref[0, 0] = rms_norm(tokens, gain_ref[...]).astype(jnp.bfloat16)
    for p in range(list_ref.shape[0]):
        meta_ref[p, 0] = list_ref[p, 0]
        for role in range(2):
            source = list_ref[p, 1 + role]
            if slots == owners:
                slot = source ^ me
            else:
                slot = jnp.int32(0)
                for j in range(owners):
                    slot = slot + jnp.where((j < source) & (route_ref[j, me] >= 0), 1, 0)
            meta_ref[p, 1 + role] = slot
            meta_ref[p, 3 + role] = len_ref[source * doc_count + jnp.maximum(route_ref[source, me], 0)]
        meta_ref[p, 5] = lax.axis_index("tensor")


def late_kernel(count, *refs):
    arrived, gain_ref = refs[:count], refs[count]
    raw_ref, late_ref = refs[count + 1 :]
    skip = count - late_ref.shape[0]
    for k in range(count):
        raw_ref[k] = arrived[k][...]
        if k >= skip:
            late_ref[k - skip, 0] = rms_norm(arrived[k][...].astype(jnp.float32), gain_ref[...]).astype(jnp.bfloat16)


def project_kernel(lead, kept_ref, came_ref, wq_ref, wk_ref, wv_ref, *refs):
    old, (q_ref, k_ref, v_ref) = refs[: len(refs) - 3], refs[len(refs) - 3 :]
    slots, half, rows, width = kept_ref.shape
    group = half * rows
    tall = slots * group
    tokens = jnp.concatenate([kept_ref[...].reshape(tall, width), came_ref[...].reshape(tall, width)], 0)
    scale = math.log2(math.e) / math.sqrt(HEAD)
    base_q, base_kv = 0, 0
    if old:
        base_q, base_kv = old[0].shape[0] if len(old) == 3 else 0, old[-1].shape[0]
        for ref, new_ref in zip(old, (q_ref, k_ref, v_ref)[3 - len(old) :]):
            new_ref[: ref.shape[0]] = ref[...]

    def store(ref, values, first, base):
        count = slots - first
        for part in range(2):
            for s in range(count):
                begin = part * count * group + s * group
                ref[base + s, part * half : (part + 1) * half] = (
                    values[begin : begin + group].astype(jnp.bfloat16).reshape(half, rows, values.shape[1])
                )

    if lead == slots:
        q_ref[...] = jnp.zeros_like(q_ref)
    else:
        asking = tokens
        if lead:
            asking = jnp.concatenate([tokens[lead * group : tall], tokens[tall + lead * group :]], 0)
        store(q_ref, jnp.dot(asking, wq_ref[...], preferred_element_type=jnp.float32) * scale, lead, base_q)
    store(k_ref, jnp.dot(tokens, wk_ref[...], preferred_element_type=jnp.float32), 0, base_kv)
    store(v_ref, jnp.dot(tokens, wv_ref[...], preferred_element_type=jnp.float32), 0, base_kv)


def project(name, lead, kept, came, weights, old):
    slots, half, rows, width = kept.shape
    wide = weights[0].shape[1]
    have_q = old[0].shape[0] if len(old) == 3 else 0
    have_kv = old[-1].shape[0] if old else 0
    nq, nkv = max(have_q + slots - lead, 1), have_kv + slots
    shape = lambda n: bf16(n, 2 * half, rows, wide)
    return kernel_call(
        functools.partial(project_kernel, lead),
        name,
        (kept, came, *weights, *old),
        [shape(nq), shape(nkv), shape(nkv)],
        limit=32,
        flops=2 * 2 * half * rows * width * wide * (3 * slots - lead),
        moved=6 * width * wide,
    )


def attend_kernel(pair, bits, query_rows, meta, q_ref, k_ref, v_ref, wo_ref, out_ref, next_ref, ctx_ref):
    _, blocks, rows, width = q_ref.shape
    keys = blocks * rows
    for a in range(meta.shape[0]):
        for b in range(meta.shape[1]):
            next_ref[a, b] = meta[a, b]
    my_slice, query = meta[0, 5], meta[pair, 0]
    first, second = meta[pair, 1], meta[pair, 2]
    lane = lax.broadcasted_iota(jnp.int32, (1, keys), 1)
    block, row = lane // rows, lane % rows
    origin = jnp.zeros_like(lane)
    for place, bit in enumerate(bits):
        origin = origin + ((block >> place) & 1) * bit
    position = (origin ^ my_slice) * rows + row
    keep = lambda yes: jnp.where(yes, 0.0, jnp.float32(-1e30))
    bias = jnp.concatenate(
        [
            keep(position < meta[pair, 3]),
            keep(position < meta[pair, 4]),
            keep((row >= query * query_rows) & (row < (query + 1) * query_rows)),
        ],
        1,
    )

    def rows_of(ref, places, at):
        return jnp.concatenate([ref[place, :, :, at].reshape(keys, HEAD) for place in places], 0)

    ones = jnp.ones((3 * keys, HEAD), jnp.bfloat16)
    for head in range(width // HEAD):
        at = slice(head * HEAD, (head + 1) * HEAD)
        qs = rows_of(q_ref, (first, second), at)
        ks = rows_of(k_ref, (first + 1, second + 1, 0), at)
        vs = rows_of(v_ref, (first + 1, second + 1, 0), at)
        scores = lax.dot_general(qs, ks, (((1,), (1,)), ((), ())), preferred_element_type=jnp.float32) + bias
        top = jnp.max(scores, -1, keepdims=True)
        expo = jnp.exp2(scores - top).astype(jnp.bfloat16)
        mixed = jnp.dot(expo, jnp.concatenate([vs, ones], 1), preferred_element_type=jnp.float32)
        ctx_ref[:, at] = (mixed[:, :HEAD] / mixed[:, HEAD:]).astype(jnp.bfloat16)
    product = jnp.dot(ctx_ref[...], wo_ref[...], preferred_element_type=jnp.float32)
    out_ref[...] = product.astype(jnp.bfloat16).reshape(out_ref.shape)


def attend(pair, bits, query_rows, meta, q, k, v, w_output):
    _, blocks, rows, width = q.shape
    model = w_output.shape[1]
    tall = 2 * blocks * rows
    return kernel_call(
        functools.partial(attend_kernel, pair, bits, query_rows),
        "attend",
        (meta, q, k, v, w_output),
        [bf16(2, blocks, rows, model), jax.ShapeDtypeStruct(meta.shape, jnp.int32)],
        scratch=[pltpu.VMEM((tall, width), jnp.bfloat16)],
        smem=(0,),
        out_smem=(1,),
        flops=2 * tall * width * (model + 3 * tall),
        moved=2 * model * width,
        exps=width // HEAD * tall * tall * 3 // 2,
    )


def settle_kernel(pair, meta, kept_ref, came_ref, rows_ref, gain_ref, hidden_ref, ffn_ref):
    for role in range(2):
        slot = meta[pair, 1 + role]
        summed = kept_ref[role, 0].astype(jnp.float32) + came_ref[role, 0].astype(jnp.float32)
        hidden = rows_ref[slot].astype(jnp.float32) + summed
        hidden_ref[role] = hidden
        ffn_ref[role, 0] = rms_norm(hidden, gain_ref[...]).astype(jnp.bfloat16)


def settle(pair, meta, kept, came, rows, gain):
    _, _, count, width = kept.shape
    return kernel_call(
        functools.partial(settle_kernel, pair),
        "settle",
        (meta, kept, came, rows, gain),
        [jax.ShapeDtypeStruct((2, count, width), jnp.float32), bf16(2, 1, count, width)],
        smem=(0,),
    )


def expand_kernel(pair, tile, meta, kept_ref, came_ref, w_ref, *rest):
    old_ref, (out_ref,) = (rest[0] if len(rest) == 2 else None), rest[-1:]
    _, half, rows, width = kept_ref.shape
    group = half * rows
    tokens = jnp.concatenate(
        [ref[role].reshape(group, width) for role in range(2) for ref in (kept_ref, came_ref)], 0
    )

    def step(i, carry):
        at = pl.ds(pl.multiple_of(i * tile, tile), tile)
        units = jnp.maximum(jnp.dot(tokens, w_ref[:, at], preferred_element_type=jnp.float32), 0.0)
        units = units.astype(jnp.bfloat16)
        if old_ref is None:
            out_ref[:, :, at] = jnp.zeros((out_ref.shape[0], 2 * group, tile), jnp.bfloat16)
        else:
            out_ref[:, :, at] = old_ref[:, :, at]
        for role in range(2):
            slot = meta[pair, 1 + role]
            out_ref[slot, :, at] = out_ref[slot, :, at] + units[role * 2 * group : (role + 1) * 2 * group]
        return carry

    lax.fori_loop(0, w_ref.shape[1] // tile, step, 0)


def expand(pair, meta, kept, came, w_in, slots, old):
    _, half, rows, width = kept.shape
    units = w_in.shape[1]
    return kernel_call(
        functools.partial(expand_kernel, pair, min(512, units)),
        "expand",
        (meta, kept, came, w_in) + (() if old is None else (old,)),
        [bf16(slots, 2 * half * rows, units)],
        smem=(0,),
        limit=32,
        flops=2 * 4 * half * rows * width * units,
        moved=2 * width * units,
    )[0]


def shrink_kernel(begin, units_ref, w_ref, out_ref):
    slots, tall, depth = units_ref.shape
    step = out_ref.shape[-1]
    product = jnp.dot(
        units_ref[...].reshape(slots * tall, depth),
        w_ref[:, begin : begin + step],
        preferred_element_type=jnp.float32,
    )
    out_ref[...] = product.astype(jnp.bfloat16).reshape(out_ref.shape)


def shrink(begin, step, units, w_down, blocks):
    slots, tall, depth = units.shape
    return kernel_call(
        functools.partial(shrink_kernel, begin),
        "shrink",
        (units, w_down),
        [bf16(slots, blocks, tall // blocks, step)],
        limit=32,
        flops=2 * slots * tall * depth * step,
        moved=2 * depth * step,
    )[0]


def finish_kernel(pairs, columns, meta, *refs):
    hidden_refs, pieces = refs[:pairs], refs[pairs : pairs + 2 * columns]
    out_refs, acc_ref = refs[pairs + 2 * columns : -1], refs[-1]
    slots, rows, width = acc_ref.shape
    step = width // columns
    for c in range(columns):
        acc_ref[:, :, c * step : (c + 1) * step] = pieces[2 * c][:, 0].astype(jnp.float32) + pieces[2 * c + 1][
            :, 0
        ].astype(jnp.float32)
    lengths = [jnp.int32(0)] * slots
    for p in range(pairs):
        for role in range(2):
            slot = meta[p, 1 + role]
            acc_ref[slot] = acc_ref[slot] + hidden_refs[p][role]
            lengths = [jnp.where(slot == s, meta[p, 3 + role], old) for s, old in enumerate(lengths)]
    position = meta[0, 5] * rows + lax.broadcasted_iota(jnp.int32, (rows, width), 0)
    for s in range(slots):
        out_refs[s][...] = jnp.where(position < lengths[s], acc_ref[s], 0.0).astype(jnp.bfloat16)


def home_kernel(route_ref, *refs):
    blocks, out_ref, acc_ref = refs[:-2], refs[-2], refs[-1]
    me = lax.axis_index("pair")
    acc_ref[...] = jnp.zeros_like(acc_ref)
    for k, block in enumerate(blocks):
        doc = route_ref[me, me ^ k]

        @pl.when(doc >= 0)
        def add():
            acc_ref[doc] = acc_ref[doc] + block[...].astype(jnp.float32)

    out_ref[...] = acc_ref[...].astype(jnp.bfloat16)


def local(
    queries,
    documents,
    doc_len,
    route,
    pair_list,
    attn_gain,
    w_query,
    w_key,
    w_value,
    w_output,
    ffn_gain,
    w_in,
    w_down,
):
    owners = lax.axis_size("pair")
    slices = lax.axis_size("tensor")
    doc_count, doc_rows, width = documents.shape
    query_count, query_rows, _ = queries.shape
    assert query_count * query_rows == doc_rows
    pairs = pair_list.shape[0]
    slots = min(2 * pairs, owners)
    direct = slots == owners
    down_bits = [1 << i for i in range(slices.bit_length() - 1)]
    up_bits = down_bits[::-1]
    attn_gain, ffn_gain = attn_gain.reshape(1, width), ffn_gain.reshape(1, width)
    weights = (w_query, w_key, w_value)

    meta, early, *arrived = kernel_call(
        functools.partial(start_kernel, slots),
        "start",
        (route, doc_len, pair_list, documents, queries, attn_gain),
        [jax.ShapeDtypeStruct((pairs, 6), jnp.int32), bf16(1 + direct, 1, doc_rows, width)]
        + [bf16(doc_rows, width)] * owners,
        smem=(0, 1, 2),
        out_smem=(0,),
    )
    arrived = [block if k == 0 else swap(block, k, "pair") for k, block in enumerate(arrived)]
    if not direct:
        me = lax.axis_index("pair")
        taken = lax.dynamic_slice_in_dim(route, me, 1, 1)[:, 0] >= 0
        source = me ^ jnp.arange(owners, dtype=jnp.int32)
        other = jnp.arange(owners, dtype=jnp.int32)
        slot_of = jnp.sum(jnp.where((other[None, :] < source[:, None]) & taken[None, :], 1, 0), 1)
        is_taken = jnp.sum(jnp.where((other[None, :] == source[:, None]) & taken[None, :], 1, 0), 1)
        place = jnp.where(is_taken > 0, slot_of, -1)
        table = (other[:slots, None] == place[None, :]).astype(jnp.bfloat16)
        packed = jnp.einsum("sk,krd->srd", table, jnp.stack(arrived), preferred_element_type=jnp.float32)
        arrived = [packed[s].astype(jnp.bfloat16) for s in range(slots)]
    rows_own, late = kernel_call(
        functools.partial(late_kernel, slots),
        "late",
        (*arrived, attn_gain),
        [bf16(slots, doc_rows, width), bf16(slots - direct, 1, doc_rows, width)],
    )

    def spread(values):
        kept = gather_blocks(values, up_bits[:-1])
        return kept, swap(kept, up_bits[-1], "tensor")

    first = project("project_early", 1, *spread(early), weights, ())
    q, k, v = project("project_late", 0, *spread(late), weights, first if direct else first[1:])

    hidden, units = [], None
    for pair in range(pairs):
        part, meta = attend(pair, up_bits, query_rows, meta, q, k, v, w_output)
        for bit in down_bits:
            kept, came = halve(part, bit)
            if bit != down_bits[-1]:
                part = kept + came
        own, ffn = settle(pair, meta, kept, came, rows_own, ffn_gain)
        hidden.append(own)
        units = expand(pair, meta, *spread(ffn), w_in, slots, units)

    columns = 2
    step = width // columns
    pieces = []
    for c in range(columns):
        part = shrink(c * step, step, units, w_down, slices)
        for bit in down_bits:
            kept, came = halve(part, bit)
            if bit != down_bits[-1]:
                part = kept + came
        pieces += [kept, came]
    blocks = kernel_call(
        functools.partial(finish_kernel, pairs, columns),
        "finish",
        (meta, *hidden, *pieces),
        [bf16(doc_rows, width)] * slots,
        scratch=[pltpu.VMEM((slots, doc_rows, width), jnp.float32)],
        smem=(0,),
    )
    if not direct:
        packed = jnp.einsum("sk,srd->krd", table, jnp.stack(blocks), preferred_element_type=jnp.float32)
        blocks = [packed[s].astype(jnp.bfloat16) for s in range(owners)]
    blocks = [block if k == 0 else swap(block, k, "pair") for k, block in enumerate(blocks)]
    return kernel_call(
        home_kernel,
        "home",
        (route, *blocks),
        [bf16(doc_count, doc_rows, width)],
        scratch=[pltpu.VMEM((doc_count, doc_rows, width), jnp.float32)],
        smem=(0,),
    )[0]


def solution(mesh):
    placed = (
        P("pair", "tensor", None),
        P("pair", "tensor", None),
        P(),
        P(),
        P("pair", None),
        P(),
        P(None, "tensor"),
        P(None, "tensor"),
        P(None, "tensor"),
        P("tensor", None),
        P(),
        P(None, "tensor"),
        P("tensor", None),
    )
    return jax.shard_map(
        local, mesh=mesh, in_specs=placed, out_specs=P("pair", "tensor", None), check_vma=False
    )
```

```python
import functools
import math

import jax
import jax.numpy as jnp
from jax import lax
from jax.experimental import pallas as pl
from jax.experimental.pallas import tpu as pltpu
from jax.sharding import PartitionSpec as P

HEAD = 128
MIB = 1024 * 1024


def rms_norm(values, gain):
    spread = jnp.mean(values * values, -1, keepdims=True)
    return values * lax.rsqrt(spread + 1e-06) * gain


def swap(values, bit, axis):
    count = lax.axis_size(axis)
    return lax.ppermute(values, axis, [(i, i ^ bit) for i in range(count)])


def gather_blocks(values, bits):
    for bit in bits:
        values = jnp.concatenate([values, swap(values, bit, "tensor")], 1)
    return values


def halve(values, bit):
    half = values.shape[1] // 2
    return values[:, :half], swap(values[:, half:], bit, "tensor")


def tie(first, second):
    return lax.optimization_barrier((first, second))


def ignoring(kernel, at, count, *refs):
    return kernel(*refs[:at], *refs[at + count :])


def kernel_call(
    kernel, name, operands, out_shape, scratch=(), smem=(), out_smem=(), hbm=(), limit=16, flops=0, moved=0, exps=0, after=()
):
    if after:
        kernel = functools.partial(ignoring, kernel, len(operands), len(after))
    anywhere = [pl.BlockSpec(memory_space=pl.ANY)] * len(after)
    space = lambda yes, far=False: pl.BlockSpec(
        memory_space=pltpu.HBM if far else pltpu.SMEM if yes else pltpu.VMEM
    )
    return pl.pallas_call(
        kernel,
        out_shape=out_shape,
        in_specs=[space(i in smem, i in hbm) for i in range(len(operands))] + anywhere,
        out_specs=[space(i in out_smem) for i in range(len(out_shape))],
        scratch_shapes=list(scratch),
        compiler_params=pltpu.CompilerParams(vmem_limit_bytes=limit * MIB),
        cost_estimate=pl.CostEstimate(flops=flops, bytes_accessed=moved, transcendentals=exps),
        name=name,
    )(*operands, *after)


def bf16(*shape):
    return jax.ShapeDtypeStruct(shape, jnp.bfloat16)


def start_kernel(slots, route_hbm, len_hbm, list_hbm, docs_hbm, queries_hbm, meta_ref, early_ref, *refs):
    route_ref, len_ref, list_ref, docs_ref, queries_ref, sems = refs[-6:]
    send_refs = refs[:-6]
    pieces = (
        (route_hbm, route_ref),
        (docs_hbm, docs_ref),
        (queries_hbm, queries_ref),
        (len_hbm, len_ref),
        (list_hbm, list_ref),
    )
    copies = [pltpu.make_async_copy(a, b, sems.at[i]) for i, (a, b) in enumerate(pieces)]
    for copy in copies:
        copy.start()
    owners = route_ref.shape[0]
    doc_count, doc_rows, width = docs_ref.shape
    me = lax.axis_index("pair")
    copies[0].wait()
    copies[1].wait()
    for k in range(owners):
        picked = docs_ref[jnp.maximum(route_ref[me, me ^ k], 0)]
        send_refs[k][...] = picked
        if k == 0 and slots == owners:
            early_ref[1, 0] = picked
    copies[2].wait()
    asked = queries_ref[...].astype(jnp.float32).reshape(doc_rows, width)
    early_ref[0, 0] = asked.astype(jnp.bfloat16)
    copies[3].wait()
    copies[4].wait()
    for p in range(list_ref.shape[0]):
        meta_ref[p, 0] = list_ref[p, 0]
        for role in range(2):
            source = list_ref[p, 1 + role]
            if slots == owners:
                slot = source ^ me
            else:
                slot = jnp.int32(0)
                for j in range(owners):
                    slot = slot + jnp.where((j < source) & (route_ref[j, me] >= 0), 1, 0)
            meta_ref[p, 1 + role] = slot
            meta_ref[p, 3 + role] = len_ref[source * doc_count + jnp.maximum(route_ref[source, me], 0)]
        meta_ref[p, 5] = lax.axis_index("tensor")
    for k in range(owners):
        meta_ref[list_ref.shape[0], k] = route_ref[me, me ^ k]


def normed(values, gain):
    return rms_norm(values.astype(jnp.float32), gain).astype(jnp.bfloat16)


def early_kernel(kept_ref, came_ref, gain_ref, out_ref):
    for s in range(kept_ref.shape[0]):
        out_ref[s, 0] = normed(kept_ref[s, 0], gain_ref[...])
        out_ref[s, 1] = normed(came_ref[s, 0], gain_ref[...])


def late_kernel(extra, kept_ref, came_ref, *refs):
    gain_ref, raw_ref, out_ref = refs[-3:]
    for s in range(extra):
        raw_ref[s, 0] = refs[0][s + 1, 0]
        raw_ref[s, 1] = refs[1][s + 1, 0]
    for s in range(kept_ref.shape[0]):
        for part, ref in enumerate((kept_ref, came_ref)):
            raw_ref[extra + s, part] = ref[s, 0]
            out_ref[s, part] = normed(ref[s, 0], gain_ref[...])


def project_kernel(lead, kept_ref, came_ref, wq_ref, wk_ref, wv_ref, *refs):
    old, (q_ref, k_ref, v_ref) = refs[: len(refs) - 3], refs[len(refs) - 3 :]
    slots, half, rows, width = kept_ref.shape
    group = half * rows
    tall = slots * group
    tokens = jnp.concatenate([kept_ref[...].reshape(tall, width), came_ref[...].reshape(tall, width)], 0)
    scale = math.log2(math.e) / math.sqrt(HEAD)
    base_q, base_kv = 0, 0
    if old:
        base_q, base_kv = old[0].shape[0] if len(old) == 3 else 0, old[-1].shape[0]
        for ref, new_ref in zip(old, (q_ref, k_ref, v_ref)[3 - len(old) :]):
            new_ref[: ref.shape[0]] = ref[...]

    def store(ref, values, first, base):
        count = slots - first
        for part in range(2):
            for s in range(count):
                begin = part * count * group + s * group
                ref[base + s, part * half : (part + 1) * half] = (
                    values[begin : begin + group].astype(jnp.bfloat16).reshape(half, rows, values.shape[1])
                )

    if lead == slots:
        q_ref[...] = jnp.zeros_like(q_ref)
    else:
        asking = tokens
        if lead:
            asking = jnp.concatenate([tokens[lead * group : tall], tokens[tall + lead * group :]], 0)
        store(q_ref, jnp.dot(asking, wq_ref[...], preferred_element_type=jnp.float32) * scale, lead, base_q)
    store(k_ref, jnp.dot(tokens, wk_ref[...], preferred_element_type=jnp.float32), 0, base_kv)
    store(v_ref, jnp.dot(tokens, wv_ref[...], preferred_element_type=jnp.float32), 0, base_kv)


def project(name, lead, kept, came, weights, old):
    slots, half, rows, width = kept.shape
    wide = weights[0].shape[1]
    have_q = old[0].shape[0] if len(old) == 3 else 0
    have_kv = old[-1].shape[0] if old else 0
    nq, nkv = max(have_q + slots - lead, 1), have_kv + slots
    shape = lambda n: bf16(n, 2 * half, rows, wide)
    return kernel_call(
        functools.partial(project_kernel, lead),
        name,
        (kept, came, *weights, *old),
        [shape(nq), shape(nkv), shape(nkv)],
        limit=32,
        flops=2 * 2 * half * rows * width * wide * (3 * slots - lead),
        moved=6 * width * wide,
    )


def attend_kernel(bits, query_rows, owners, meta, q_ref, k_ref, v_ref, wo_ref, raw_ref, *refs):
    out_ref, rest_ref, mine_ref, role_ref, valid_ref, home_ref, ctx_ref, expo_ref = refs
    _, blocks, rows, width = q_ref.shape
    pairs = meta.shape[0] - 1
    slots = valid_ref.shape[0]
    flag = lambda yes: jnp.full((8, 128), yes.astype(jnp.float32), jnp.float32)
    place = lax.broadcasted_iota(jnp.int32, (rows, 128), 0) + meta[0, 5] * rows
    lengths = [jnp.int32(0)] * slots
    for p in range(pairs):
        for role in range(2):
            slot = meta[p, 1 + role]
            mine_ref[p, role] = raw_ref[slot]
            for s in range(slots):
                role_ref[2 * p + role, s] = flag(slot == s)
                lengths[s] = jnp.where(slot == s, meta[p, 3 + role], lengths[s])
    for s in range(slots):
        valid_ref[s] = (place < lengths[s]).astype(jnp.float32)
    for d in range(home_ref.shape[0]):
        for k in range(owners):
            home_ref[d, k] = flag(meta[pairs, k] == d)
    keys = blocks * rows
    heads = width // HEAD
    lane = lax.broadcasted_iota(jnp.int32, (1, keys), 1)
    block, row = lane // rows, lane % rows
    origin = jnp.zeros_like(lane)
    for place, bit in enumerate(bits):
        origin = origin + ((block >> place) & 1) * bit
    position = (origin ^ meta[0, 5]) * rows + row
    keep = lambda yes: jnp.where(yes, 0.0, jnp.float32(-1e30))
    ones = jnp.ones((3 * keys, HEAD), jnp.bfloat16)

    def rows_of(ref, places, at):
        return jnp.concatenate([ref[place, :, :, at].reshape(keys, HEAD) for place in places], 0)

    def one_pair(pair, carry):
        query, first, second = meta[pair, 0], meta[pair, 1], meta[pair, 2]
        bias = jnp.concatenate(
            [
                keep(position < meta[pair, 3]),
                keep(position < meta[pair, 4]),
                keep((row >= query * query_rows) & (row < (query + 1) * query_rows)),
            ],
            1,
        )
        for head in range(heads):
            at = slice(head * HEAD, (head + 1) * HEAD)
            qs = rows_of(q_ref, (first, second), at)
            ks = rows_of(k_ref, (first + 1, second + 1, 0), at)
            scores = lax.dot_general(qs, ks, (((1,), (1,)), ((), ())), preferred_element_type=jnp.float32) + bias
            top = jnp.max(scores, -1, keepdims=True)
            expo_ref[head] = jnp.exp2(scores - top).astype(jnp.bfloat16)
        for head in range(heads):
            at = slice(head * HEAD, (head + 1) * HEAD)
            vs = rows_of(v_ref, (first + 1, second + 1, 0), at)
            mixed = jnp.dot(expo_ref[head], jnp.concatenate([vs, ones], 1), preferred_element_type=jnp.float32)
            ctx_ref[pl.ds(pl.multiple_of(pair * 2 * keys, 2 * keys), 2 * keys), at] = (
                mixed[:, :HEAD] / mixed[:, HEAD:]
            ).astype(jnp.bfloat16)
        return carry

    lax.fori_loop(0, pairs, one_pair, 0)
    begin = out_ref.shape[0] * keys
    product = jnp.dot(ctx_ref[:begin], wo_ref[...], preferred_element_type=jnp.float32)
    out_ref[...] = product.astype(jnp.bfloat16).reshape(out_ref.shape)
    if begin < ctx_ref.shape[0]:
        rest_ref[...] = ctx_ref[begin:]


def attend(lead, bits, query_rows, doc_count, owners, meta, q, k, v, w_output, raw):
    _, blocks, rows, width = q.shape
    pairs, model, slots = meta.shape[0] - 1, w_output.shape[1], raw.shape[0]
    f32 = lambda *shape: jax.ShapeDtypeStruct(shape, jnp.float32)
    tall = 2 * blocks * rows
    return kernel_call(
        functools.partial(attend_kernel, bits, query_rows, owners),
        "attend",
        (meta, q, k, v, w_output, raw),
        [
            bf16(2 * lead, blocks, rows, model),
            bf16(max(pairs - lead, 1) * tall, width),
            bf16(pairs, 2, *raw.shape[1:]),
            f32(2 * pairs, slots, 8, 128),
            f32(slots, rows, 128),
            f32(doc_count, owners, 8, 128),
        ],
        scratch=[
            pltpu.VMEM((pairs * tall, width), jnp.bfloat16),
            pltpu.VMEM((width // HEAD, tall, tall * 3 // 2), jnp.bfloat16),
        ],
        smem=(0,),
        flops=2 * tall * width * (model + 3 * pairs * tall),
        moved=2 * model * width,
        exps=pairs * width // HEAD * tall * tall * 3 // 2,
    )


def output_kernel(groups, ctx_ref, wo_ref, *out_refs):
    product = jnp.dot(ctx_ref[...], wo_ref[...], preferred_element_type=jnp.float32).astype(jnp.bfloat16)
    tall = ctx_ref.shape[0] // sum(groups)
    for i, out_ref in enumerate(out_refs):
        begin = sum(groups[:i])
        out_ref[...] = product[begin * tall : (begin + groups[i]) * tall].reshape(out_ref.shape)


def settle_kernel(pair, kept_ref, came_ref, mine_ref, gain_ref, hidden_ref, ffn_ref):
    for role in range(kept_ref.shape[0]):
        for part in range(2):
            summed = kept_ref[role, part].astype(jnp.float32) + came_ref[role, 1 - part].astype(jnp.float32)
            hidden = mine_ref[pair + role // 2, role % 2, part].astype(jnp.float32) + summed
            if part == 0:
                hidden_ref[role] = hidden
            ffn_ref[role, part] = rms_norm(hidden, gain_ref[...]).astype(jnp.bfloat16)


def settle(pair, kept, came, mine, gain):
    roles, _, count, width = kept.shape
    return kernel_call(
        functools.partial(settle_kernel, pair),
        "settle",
        (kept, came, mine, gain),
        [jax.ShapeDtypeStruct((roles, count, width), jnp.float32), bf16(roles, 2, count, width)],
    )


def expand_kernel(pairs, tile, meta, w_ref, *refs):
    pieces, out_ref = refs[:-1], refs[-1]
    _, half, rows, width = pieces[0].shape
    group = half * rows
    tokens = jnp.concatenate(
        [
            pieces[i + part][role].reshape(group, width)
            for i in range(0, len(pieces), 2)
            for role in range(pieces[i].shape[0])
            for part in range(2)
        ],
        0,
    )

    def step(i, carry):
        at = pl.ds(pl.multiple_of(i * tile, tile), tile)
        units = jnp.maximum(jnp.dot(tokens, w_ref[:, at], preferred_element_type=jnp.float32), 0.0)
        units = units.astype(jnp.bfloat16)
        out_ref[:, :, at] = jnp.zeros((out_ref.shape[0], 2 * group, tile), jnp.bfloat16)
        for r in range(2 * pairs):
            slot = meta[r // 2, 1 + r % 2]
            out_ref[slot, :, at] = out_ref[slot, :, at] + units[r * 2 * group : (r + 1) * 2 * group]
        return carry

    lax.fori_loop(0, w_ref.shape[1] // tile, step, 0, unroll=2)


def expand(meta, pieces, w_in, slots):
    _, half, rows, width = pieces[0].shape
    units = w_in.shape[1]
    pairs = sum(piece.shape[0] for piece in pieces) // 4
    return kernel_call(
        functools.partial(expand_kernel, pairs, min(512, units)),
        "expand",
        (meta, w_in, *pieces),
        [bf16(slots, 2 * half * rows, units)],
        smem=(0,),
        limit=24,
        flops=2 * pairs * 4 * half * rows * width * units,
        moved=2 * width * units,
    )[0]


def shrink_kernel(low, high, begin, units_ref, w_ref, out_ref):
    _, tall, depth = units_ref.shape
    step = out_ref.shape[-1]
    product = jnp.dot(
        units_ref[low:high].reshape((high - low) * tall, depth),
        w_ref[:, begin : begin + step],
        preferred_element_type=jnp.float32,
    )
    out_ref[...] = product.astype(jnp.bfloat16).reshape(out_ref.shape)


def shrink(low, high, begin, step, units, w_down, blocks, after):
    _, tall, depth = units.shape
    return kernel_call(
        functools.partial(shrink_kernel, low, high, begin),
        "shrink",
        (units, w_down),
        [bf16(high - low, blocks, tall // blocks, step)],
        limit=24,
        flops=2 * (high - low) * tall * depth * step,
        moved=2 * depth * step,
        after=after,
    )[0]


def wide(flags, width):
    return jnp.concatenate([flags] * (width // 128), 1)


def finish_kernel(low, columns, role_ref, valid_ref, hidden_ref, *refs):
    pieces, out_refs = refs[: 2 * columns], refs[2 * columns :]
    roles, rows, width = hidden_ref.shape
    for i, out_ref in enumerate(out_refs):
        total = jnp.concatenate(
            [
                pieces[2 * c][i, 0].astype(jnp.float32) + pieces[2 * c + 1][i, 0].astype(jnp.float32)
                for c in range(columns)
            ],
            1,
        )
        for r in range(roles):
            chosen = jnp.concatenate([wide(role_ref[r, low + i], width)] * (rows // 8), 0)
            total = total + jnp.where(chosen > 0.0, hidden_ref[r], 0.0)
        valid = wide(valid_ref[low + i], width) > 0.0
        out_ref[...] = jnp.where(valid, total, 0.0).astype(jnp.bfloat16)


def home_kernel(home_ref, *refs):
    blocks, out_ref = refs[:-1], refs[-1]
    rows, width = blocks[0].shape
    for d in range(out_ref.shape[0]):
        total = jnp.zeros((rows, width), jnp.float32)
        for k, block in enumerate(blocks):
            chosen = jnp.concatenate([wide(home_ref[d, k], width)] * (rows // 8), 0)
            total = total + jnp.where(chosen > 0.0, block[...].astype(jnp.float32), 0.0)
        out_ref[d] = total.astype(jnp.bfloat16)


def local(
    queries,
    documents,
    doc_len,
    route,
    pair_list,
    attn_gain,
    w_query,
    w_key,
    w_value,
    w_output,
    ffn_gain,
    w_in,
    w_down,
):
    owners = lax.axis_size("pair")
    slices = lax.axis_size("tensor")
    doc_count, doc_rows, width = documents.shape
    query_count, query_rows, _ = queries.shape
    assert query_count * query_rows == doc_rows
    pairs = pair_list.shape[0]
    slots = min(2 * pairs, owners)
    direct = slots == owners
    down_bits = [1 << i for i in range(slices.bit_length() - 1)]
    up_bits = down_bits[::-1]
    attn_gain, ffn_gain = attn_gain.reshape(1, width), ffn_gain.reshape(1, width)
    weights = (w_query, w_key, w_value)

    meta, early, *arrived = kernel_call(
        functools.partial(start_kernel, slots),
        "start",
        (route, doc_len, pair_list, documents, queries),
        [jax.ShapeDtypeStruct((pairs + 1, max(6, owners)), jnp.int32), bf16(1 + direct, 1, doc_rows, width)]
        + [bf16(doc_rows, width)] * owners,
        scratch=[
            pltpu.SMEM(route.shape, jnp.int32),
            pltpu.SMEM(doc_len.shape, jnp.int32),
            pltpu.SMEM(pair_list.shape, jnp.int32),
            pltpu.VMEM(documents.shape, jnp.bfloat16),
            pltpu.VMEM(queries.shape, jnp.bfloat16),
            pltpu.SemaphoreType.DMA((5,)),
        ],
        hbm=(0, 1, 2, 3, 4),
        out_smem=(0,),
        limit=63,
        flops=8 * 10**9,
    )
    arrived = [block if k == 0 else swap(block, k, "pair") for k, block in enumerate(arrived)]
    if not direct:
        me = lax.axis_index("pair")
        taken = lax.dynamic_slice_in_dim(route, me, 1, 1)[:, 0] >= 0
        source = me ^ jnp.arange(owners, dtype=jnp.int32)
        other = jnp.arange(owners, dtype=jnp.int32)
        slot_of = jnp.sum(jnp.where((other[None, :] < source[:, None]) & taken[None, :], 1, 0), 1)
        is_taken = jnp.sum(jnp.where((other[None, :] == source[:, None]) & taken[None, :], 1, 0), 1)
        place = jnp.where(is_taken > 0, slot_of, -1)
        table = (other[:slots, None] == place[None, :]).astype(jnp.bfloat16)
        packed = jnp.einsum("sk,krd->srd", table, jnp.stack(arrived), preferred_element_type=jnp.float32)
        arrived = [packed[s].astype(jnp.bfloat16) for s in range(slots)]
    top = up_bits[0]
    pairwise = lambda a: bf16(a.shape[0], 2, doc_rows, width)
    early_came = swap(early, top, "tensor")
    early_norm = kernel_call(early_kernel, "early", (early, early_came, attn_gain), [pairwise(early)], flops=8 * 10**9)[0]
    late = jnp.stack(arrived[direct:])[:, None]
    late, early_norm = tie(late, early_norm)
    late_came = swap(late, top, "tensor")
    more = (early, early_came) if direct else ()
    rows_own, late_norm = kernel_call(
        functools.partial(late_kernel, int(direct)),
        "late",
        (late, late_came, *more, attn_gain),
        [bf16(slots, 2, doc_rows, width), pairwise(late)],
        flops=8 * 10**9,
    )

    def spread(kept):
        return kept, swap(kept, up_bits[-1], "tensor")

    early_kept = gather_blocks(early_norm, up_bits[1:-1])
    first = project("project_early", 1, *spread(early_kept), weights, ())
    late_kept = gather_blocks(late_norm, up_bits[1:-1])
    late_kept, first = tie(late_kept, first)
    q, k, v = project("project_late", 0, *spread(late_kept), weights, first if direct else first[1:])

    groups = [1] * pairs
    part, rest, mine, roles, valid, homes = attend(
        groups[0], up_bits, query_rows, doc_count, owners, meta, q, k, v, w_output, rows_own
    )
    parts = [part]
    if groups[1:]:
        parts += kernel_call(
            functools.partial(output_kernel, groups[1:]),
            "output",
            (rest, w_output),
            [bf16(2 * n, *part.shape[1:]) for n in groups[1:]],
            flops=2 * rest.size * width,
            moved=2 * w_output.size,
        )
    hidden, pieces = [], []
    for group, part in enumerate(parts):
        for bit in down_bits[:-1]:
            kept, came = halve(part, bit)
            part = kept + came
        came = swap(part, down_bits[-1], "tensor")
        own, ffn = settle(sum(groups[:group]), part, came, mine, ffn_gain)
        hidden.append(own)
        pieces += spread(gather_blocks(ffn, up_bits[1:-1]))
    units = expand(meta, pieces, w_in, slots)
    hidden = jnp.concatenate(hidden, 0)

    def shrunk(low, high, columns, after=()):
        step = width // columns
        return [shrink(low, high, c * step, step, units, w_down, slices, after) for c in range(columns)]

    def reduce(parts, low, high):
        columns = len(parts)
        pieces = []
        for part in parts:
            for bit in down_bits:
                kept, came = halve(part, bit)
                if bit != down_bits[-1]:
                    part = kept + came
            pieces += [kept, came]
        return kernel_call(
            functools.partial(finish_kernel, low, columns),
            "finish",
            (roles, valid, hidden, *pieces),
            [bf16(doc_rows, width)] * (high - low),
        )

    blocks = reduce(shrunk(0, slots, 2), 0, slots)
    if not direct:
        packed = jnp.einsum("sk,srd->krd", table, jnp.stack(blocks), preferred_element_type=jnp.float32)
        blocks = [packed[s].astype(jnp.bfloat16) for s in range(owners)]
    blocks = [block if k == 0 else swap(block, k, "pair") for k, block in enumerate(blocks)]
    return kernel_call(home_kernel, "home", (homes, *blocks), [bf16(doc_count, doc_rows, width)])[0]


def solution(mesh):
    placed = (
        P("pair", "tensor", None),
        P("pair", "tensor", None),
        P(),
        P(),
        P("pair", None),
        P(),
        P(None, "tensor"),
        P(None, "tensor"),
        P(None, "tensor"),
        P("tensor", None),
        P(),
        P(None, "tensor"),
        P("tensor", None),
    )
    return jax.shard_map(
        local, mesh=mesh, in_specs=placed, out_specs=P("pair", "tensor", None), check_vma=False
    )
```

```python
import functools
import math

import jax
import jax.numpy as jnp
from jax import lax
from jax.experimental import pallas as pl
from jax.experimental.pallas import tpu as pltpu
from jax.sharding import PartitionSpec as P

HEAD = 128
MIB = 1024 * 1024
WAIT = 8 * 10**9


def rms_norm(values, gain):
    spread = jnp.mean(values * values, -1, keepdims=True)
    return values * lax.rsqrt(spread + 1e-06) * gain


def swap(values, bit, axis):
    count = lax.axis_size(axis)
    return lax.ppermute(values, axis, [(i, i ^ bit) for i in range(count)])


def gather_blocks(values, bits):
    for bit in bits:
        values = jnp.concatenate([values, swap(values, bit, "tensor")], 1)
    return values


def halve(values, bit):
    half = values.shape[1] // 2
    return values[:, :half], swap(values[:, half:], bit, "tensor")


def tie(first, second):
    return lax.optimization_barrier((first, second))


def ignoring(kernel, at, count, *refs):
    return kernel(*refs[:at], *refs[at + count :])


def kernel_call(
    kernel, name, operands, out_shape, scratch=(), smem=(), out_smem=(), hbm=(), limit=16, flops=0, moved=0, exps=0, after=()
):
    if after:
        kernel = functools.partial(ignoring, kernel, len(operands), len(after))
    anywhere = [pl.BlockSpec(memory_space=pl.ANY)] * len(after)
    space = lambda yes, far=False: pl.BlockSpec(
        memory_space=pltpu.HBM if far else pltpu.SMEM if yes else pltpu.VMEM
    )
    return pl.pallas_call(
        kernel,
        out_shape=out_shape,
        in_specs=[space(i in smem, i in hbm) for i in range(len(operands))] + anywhere,
        out_specs=[space(i in out_smem) for i in range(len(out_shape))],
        scratch_shapes=list(scratch),
        compiler_params=pltpu.CompilerParams(vmem_limit_bytes=limit * MIB),
        cost_estimate=pl.CostEstimate(flops=flops, bytes_accessed=moved, transcendentals=exps),
        name=name,
    )(*operands, *after)


def bf16(*shape):
    return jax.ShapeDtypeStruct(shape, jnp.bfloat16)


def start_kernel(slots, route_hbm, len_hbm, list_hbm, docs_hbm, queries_hbm, meta_ref, early_ref, *refs):
    route_ref, len_ref, list_ref, docs_ref, queries_ref, sems = refs[-6:]
    send_refs = refs[:-6]
    pieces = (
        (route_hbm, route_ref),
        (docs_hbm, docs_ref),
        (queries_hbm, queries_ref),
        (len_hbm, len_ref),
        (list_hbm, list_ref),
    )
    copies = [pltpu.make_async_copy(a, b, sems.at[i]) for i, (a, b) in enumerate(pieces)]
    for copy in copies:
        copy.start()
    owners = route_ref.shape[0]
    doc_count, doc_rows, width = docs_ref.shape
    me = lax.axis_index("pair")
    copies[0].wait()
    copies[1].wait()
    for k in range(owners):
        picked = docs_ref[jnp.maximum(route_ref[me, me ^ k], 0)]
        send_refs[k][...] = picked
        if k == 0 and slots == owners:
            early_ref[1, 0] = picked
    copies[2].wait()
    asked = queries_ref[...].astype(jnp.float32).reshape(doc_rows, width)
    early_ref[0, 0] = asked.astype(jnp.bfloat16)
    copies[3].wait()
    copies[4].wait()
    for p in range(list_ref.shape[0]):
        meta_ref[p, 0] = list_ref[p, 0]
        for role in range(2):
            source = list_ref[p, 1 + role]
            if slots == owners:
                slot = source ^ me
            else:
                slot = jnp.int32(0)
                for j in range(owners):
                    slot = slot + jnp.where((j < source) & (route_ref[j, me] >= 0), 1, 0)
            meta_ref[p, 1 + role] = slot
            meta_ref[p, 3 + role] = len_ref[source * doc_count + jnp.maximum(route_ref[source, me], 0)]
        meta_ref[p, 5] = lax.axis_index("tensor")
    for k in range(owners):
        meta_ref[list_ref.shape[0], k] = route_ref[me, me ^ k]


def normed(values, gain):
    return rms_norm(values.astype(jnp.float32), gain).astype(jnp.bfloat16)


def stack_kernel(*refs):
    for i, ref in enumerate(refs[:-1]):
        refs[-1][i, 0] = ref[...]


def join_kernel(kept_ref, came_ref, out_ref):
    out_ref[:, :1] = kept_ref[...]
    out_ref[:, 1:] = came_ref[...]


def join(kept, came):
    slots, _, rows, width = kept.shape
    return kernel_call(join_kernel, "join", (kept, came), [bf16(slots, 2, rows, width)], flops=WAIT)[0]


def project_kernel(lead, kept_ref, came_ref, gain_ref, wq_ref, wk_ref, wv_ref, *refs):
    old, (q_ref, k_ref, v_ref) = refs[: len(refs) - 3], refs[len(refs) - 3 :]
    slots, half, rows, width = kept_ref.shape
    group = half * rows
    tall = slots * group
    tokens = jnp.concatenate([kept_ref[...].reshape(tall, width), came_ref[...].reshape(tall, width)], 0)
    tokens = normed(tokens, gain_ref[...])
    scale = math.log2(math.e) / math.sqrt(HEAD)
    base_q, base_kv = 0, 0
    if old:
        base_q, base_kv = old[0].shape[0] if len(old) == 3 else 0, old[-1].shape[0]
        for ref, new_ref in zip(old, (q_ref, k_ref, v_ref)[3 - len(old) :]):
            new_ref[: ref.shape[0]] = ref[...]

    def store(ref, values, first, base):
        count = slots - first
        for part in range(2):
            for s in range(count):
                begin = part * count * group + s * group
                ref[base + s, part * half : (part + 1) * half] = (
                    values[begin : begin + group].astype(jnp.bfloat16).reshape(half, rows, values.shape[1])
                )

    if lead == slots:
        q_ref[...] = jnp.zeros_like(q_ref)
    else:
        asking = tokens
        if lead:
            asking = jnp.concatenate([tokens[lead * group : tall], tokens[tall + lead * group :]], 0)
        store(q_ref, jnp.dot(asking, wq_ref[...], preferred_element_type=jnp.float32) * scale, lead, base_q)
    store(k_ref, jnp.dot(tokens, wk_ref[...], preferred_element_type=jnp.float32), 0, base_kv)
    store(v_ref, jnp.dot(tokens, wv_ref[...], preferred_element_type=jnp.float32), 0, base_kv)


def project(name, lead, kept, came, gain, weights, old):
    slots, half, rows, width = kept.shape
    wide = weights[0].shape[1]
    have_q = old[0].shape[0] if len(old) == 3 else 0
    have_kv = old[-1].shape[0] if old else 0
    nq, nkv = max(have_q + slots - lead, 1), have_kv + slots
    shape = lambda n: bf16(n, 2 * half, rows, wide)
    return kernel_call(
        functools.partial(project_kernel, lead),
        name,
        (kept, came, gain, *weights, *old),
        [shape(nq), shape(nkv), shape(nkv)],
        limit=32,
        flops=2 * 2 * half * rows * width * wide * (3 * slots - lead),
        moved=6 * width * wide,
    )


def project_part_kernel(scale, rows_ref, gain_ref, wq_ref, wk_ref, wv_ref, *refs):
    olds, outs = refs[:-3], refs[-3:]
    slots, half, rows, width = rows_ref.shape
    tokens = normed(rows_ref[...].reshape(slots * half * rows, width), gain_ref[...])
    kept, ahead = olds[:3], (None,) * (6 - len(olds)) + olds[3:] if olds else ()
    for i, (w_ref, out_ref) in enumerate(zip((wq_ref, wk_ref, wv_ref), outs)):
        values = jnp.dot(tokens, w_ref[...], preferred_element_type=jnp.float32)
        if i == 0:
            values = values * scale
        values = values.astype(jnp.bfloat16).reshape(slots, half, rows, values.shape[1])
        if not olds:
            out_ref[...] = values
            continue
        base = out_ref.shape[0] - slots
        if base:
            out_ref[:base] = ahead[i][...]
        out_ref[base:, :half] = kept[i][...]
        out_ref[base:, half:] = values


def project_part(name, rows_in, gain, weights, kept=(), ahead=()):
    slots, half, rows, width = rows_in.shape
    wide = weights[0].shape[1]
    bases = (0,) * (3 - len(ahead)) + tuple(a.shape[0] for a in ahead)
    return kernel_call(
        functools.partial(project_part_kernel, math.log2(math.e) / math.sqrt(HEAD)),
        name,
        (rows_in, gain, *weights, *kept, *ahead),
        [bf16(base + slots, half * (2 if kept else 1), rows, wide) for base in bases],
        limit=24,
        flops=6 * slots * half * rows * width * wide,
        moved=6 * width * wide,
    )


def attend_kernel(bits, query_rows, owners, others, direct, meta, q_ref, k_ref, v_ref, wo_ref, late_ref, *refs):
    early_ref, refs = (refs[0], refs[1:]) if direct else (None, refs)
    out_ref, rest_ref, mine_ref, role_ref, valid_ref, home_ref, ctx_ref, expo_ref = refs
    _, blocks, rows, width = q_ref.shape
    pairs = meta.shape[0] - 1
    slots = valid_ref.shape[0]
    flag = lambda yes: jnp.full((8, 128), yes.astype(jnp.float32), jnp.float32)
    place = lax.broadcasted_iota(jnp.int32, (rows, 128), 0) + meta[0, 5] * rows
    lengths = [jnp.int32(0)] * slots
    for p in range(pairs):
        for role in range(2):
            slot = meta[p, 1 + role]
            for part, at in enumerate((0, others[p])):
                if direct:
                    chosen = late_ref[jnp.maximum(slot - 1, 0), at]
                    mine_ref[p, role, part] = jnp.where(slot == 0, early_ref[1, at], chosen)
                else:
                    mine_ref[p, role, part] = late_ref[slot, at]
            for s in range(slots):
                role_ref[2 * p + role, s] = flag(slot == s)
                lengths[s] = jnp.where(slot == s, meta[p, 3 + role], lengths[s])
    for s in range(slots):
        valid_ref[s] = (place < lengths[s]).astype(jnp.float32)
    for d in range(home_ref.shape[0]):
        for k in range(owners):
            home_ref[d, k] = flag(meta[pairs, k] == d)
    keys = blocks * rows
    heads = width // HEAD
    lane = lax.broadcasted_iota(jnp.int32, (1, keys), 1)
    block, row = lane // rows, lane % rows
    origin = jnp.zeros_like(lane)
    for place, bit in enumerate(bits):
        origin = origin + ((block >> place) & 1) * bit
    position = (origin ^ meta[0, 5]) * rows + row
    keep = lambda yes: jnp.where(yes, 0.0, jnp.float32(-1e30))
    ones = jnp.ones((3 * keys, HEAD), jnp.bfloat16)

    def rows_of(ref, places, at):
        return jnp.concatenate([ref[place, :, :, at].reshape(keys, HEAD) for place in places], 0)

    def one_pair(pair, carry):
        query, first, second = meta[pair, 0], meta[pair, 1], meta[pair, 2]
        bias = jnp.concatenate(
            [
                keep(position < meta[pair, 3]),
                keep(position < meta[pair, 4]),
                keep((row >= query * query_rows) & (row < (query + 1) * query_rows)),
            ],
            1,
        )
        for head in range(heads):
            at = slice(head * HEAD, (head + 1) * HEAD)
            qs = rows_of(q_ref, (first, second), at)
            ks = rows_of(k_ref, (first + 1, second + 1, 0), at)
            scores = lax.dot_general(qs, ks, (((1,), (1,)), ((), ())), preferred_element_type=jnp.float32) + bias
            top = jnp.max(scores, -1, keepdims=True)
            expo_ref[head] = jnp.exp2(scores - top).astype(jnp.bfloat16)
        for head in range(heads):
            at = slice(head * HEAD, (head + 1) * HEAD)
            vs = rows_of(v_ref, (first + 1, second + 1, 0), at)
            mixed = jnp.dot(expo_ref[head], jnp.concatenate([vs, ones], 1), preferred_element_type=jnp.float32)
            ctx_ref[pl.ds(pl.multiple_of(pair * 2 * keys, 2 * keys), 2 * keys), at] = (
                mixed[:, :HEAD] / mixed[:, HEAD:]
            ).astype(jnp.bfloat16)
        return carry

    lax.fori_loop(0, pairs, one_pair, 0)
    begin = out_ref.shape[0] * keys
    product = jnp.dot(ctx_ref[:begin], wo_ref[...], preferred_element_type=jnp.float32)
    out_ref[...] = product.astype(jnp.bfloat16).reshape(out_ref.shape)
    if begin < ctx_ref.shape[0]:
        rest_ref[...] = ctx_ref[begin:]


def attend(groups, swapped, bits, query_rows, doc_count, owners, meta, q, k, v, w_output, late, early):
    _, blocks, rows, width = q.shape
    pairs, model, slots, lead = meta.shape[0] - 1, w_output.shape[1], q.shape[0], groups[0]
    others = [late.shape[1] // 2 if far else 1 for n, far in zip(groups, swapped) for _ in range(n)]
    f32 = lambda *shape: jax.ShapeDtypeStruct(shape, jnp.float32)
    tall = 2 * blocks * rows
    return kernel_call(
        functools.partial(attend_kernel, bits, query_rows, owners, others, early is not None),
        "attend",
        (meta, q, k, v, w_output, late) + (() if early is None else (early,)),
        [
            bf16(2 * lead, blocks, rows, model),
            bf16(max(pairs - lead, 1) * tall, width),
            bf16(pairs, 2, 2, *late.shape[2:]),
            f32(2 * pairs, slots, 8, 128),
            f32(slots, rows, 128),
            f32(doc_count, owners, 8, 128),
        ],
        scratch=[
            pltpu.VMEM((pairs * tall, width), jnp.bfloat16),
            pltpu.VMEM((width // HEAD, tall, tall * 3 // 2), jnp.bfloat16),
        ],
        smem=(0,),
        flops=2 * tall * width * (model + 3 * pairs * tall),
        moved=2 * model * width,
        exps=pairs * width // HEAD * tall * tall * 3 // 2,
    )


def turned(blocks):
    bits = blocks.bit_length() - 1
    return [sum(((b >> i) & 1) << (bits - 1 - i) for i in range(bits)) for b in range(blocks)]


def output_kernel(groups, swapped, ctx_ref, wo_ref, *out_refs):
    product = jnp.dot(ctx_ref[...], wo_ref[...], preferred_element_type=jnp.float32).astype(jnp.bfloat16)
    tall = ctx_ref.shape[0] // sum(groups)
    for i, out_ref in enumerate(out_refs):
        begin = sum(groups[:i])
        values = product[begin * tall : (begin + groups[i]) * tall].reshape(out_ref.shape)
        if not swapped[i]:
            out_ref[...] = values
            continue
        half = out_ref.shape[1] // 2
        for b, to in enumerate(turned(half)):
            out_ref[:, to] = values[:, b]
            out_ref[:, half + to] = values[:, half + b]


def settle_kernel(pair, kept_ref, came_ref, mine_ref, gain_ref, hidden_ref, ffn_ref):
    for role in range(kept_ref.shape[0]):
        for part in range(2):
            summed = kept_ref[role, part].astype(jnp.float32) + came_ref[role, 1 - part].astype(jnp.float32)
            hidden = mine_ref[pair + role // 2, role % 2, part].astype(jnp.float32) + summed
            if part == 0:
                hidden_ref[role] = hidden
            ffn_ref[role, part] = rms_norm(hidden, gain_ref[...]).astype(jnp.bfloat16)


def settle(pair, kept, came, mine, gain):
    roles, _, count, width = kept.shape
    return kernel_call(
        functools.partial(settle_kernel, pair),
        "settle",
        (kept, came, mine, gain),
        [jax.ShapeDtypeStruct((roles, count, width), jnp.float32), bf16(roles, 2, count, width)],
    )


def expand_kernel(swapped, tile, meta, w_ref, *refs):
    pieces, rest = refs[: len(swapped)], refs[len(swapped) :]
    old_ref, out_ref = (rest[0] if len(rest) == 2 else None), rest[-1]
    _, half, rows, width = pieces[0].shape
    group = half * rows
    tokens = []
    for piece, far in zip(pieces, swapped):
        for r in range(piece.shape[0]):
            if far:
                tokens += [piece[r, b] for b in turned(half)]
            else:
                tokens.append(piece[r].reshape(group, width))
    tokens = jnp.concatenate(tokens, 0)
    last = out_ref.shape[0] - 1

    def step(i, carry):
        at = pl.ds(pl.multiple_of(i * tile, tile), tile)
        units = jnp.maximum(jnp.dot(tokens, w_ref[:, at], preferred_element_type=jnp.float32), 0.0)
        units = units.astype(jnp.bfloat16)
        if old_ref is not None:
            out_ref[0, :, :, at] = old_ref[0, :, :, at]
        out_ref[last, :, :, at] = jnp.zeros((out_ref.shape[1], group, tile), jnp.bfloat16)
        for r in range(tokens.shape[0] // group):
            slot = meta[r // 2, 1 + r % 2]
            out_ref[last, slot, :, at] = out_ref[last, slot, :, at] + units[r * group : (r + 1) * group]
        return carry

    lax.fori_loop(0, w_ref.shape[1] // tile, step, 0, unroll=2)


def expand(meta, swapped, pieces, w_in, slots, old=()):
    _, half, rows, width = pieces[0].shape
    units = w_in.shape[1]
    roles = sum(piece.shape[0] for piece in pieces)
    return kernel_call(
        functools.partial(expand_kernel, swapped, min(512, units)),
        "expand",
        (meta, w_in, *pieces, *old),
        [bf16(1 + len(old), slots, half * rows, units)],
        smem=(0,),
        limit=24,
        flops=2 * roles * half * rows * width * units,
        moved=2 * width * units,
    )


def shrink_kernel(begin, units_ref, w_ref, out_ref):
    parts, slots, tall, depth = units_ref.shape
    _, blocks, rows, step = out_ref.shape
    product = jnp.dot(
        units_ref[...].reshape(parts * slots * tall, depth),
        w_ref[:, begin : begin + step],
        preferred_element_type=jnp.float32,
    )
    product = product.astype(jnp.bfloat16).reshape(parts, slots, blocks // parts, rows, step)
    for part in range(parts):
        out_ref[:, part * (blocks // parts) : (part + 1) * (blocks // parts)] = product[part]


def shrink(begin, step, units, w_down, blocks):
    parts, slots, tall, depth = units.shape
    return kernel_call(
        functools.partial(shrink_kernel, begin),
        "shrink",
        (units, w_down),
        [bf16(slots, blocks, parts * tall // blocks, step)],
        limit=24,
        flops=2 * parts * slots * tall * depth * step,
        moved=2 * depth * step,
    )[0]


def wide(flags, width):
    return jnp.concatenate([flags] * (width // 128), 1)


def finish_kernel(low, columns, role_ref, valid_ref, hidden_ref, *refs):
    pieces, out_refs = refs[: 2 * columns], refs[2 * columns :]
    roles, rows, width = hidden_ref.shape
    for i, out_ref in enumerate(out_refs):
        total = jnp.concatenate(
            [
                pieces[2 * c][i, 0].astype(jnp.float32) + pieces[2 * c + 1][i, 0].astype(jnp.float32)
                for c in range(columns)
            ],
            1,
        )
        for r in range(roles):
            chosen = jnp.concatenate([wide(role_ref[r, low + i], width)] * (rows // 8), 0)
            total = total + jnp.where(chosen > 0.0, hidden_ref[r], 0.0)
        valid = wide(valid_ref[low + i], width) > 0.0
        out_ref[...] = jnp.where(valid, total, 0.0).astype(jnp.bfloat16)


def home_kernel(home_ref, *refs):
    blocks, out_ref = refs[:-1], refs[-1]
    rows, width = blocks[0].shape
    for d in range(out_ref.shape[0]):
        total = jnp.zeros((rows, width), jnp.float32)
        for k, block in enumerate(blocks):
            chosen = jnp.concatenate([wide(home_ref[d, k], width)] * (rows // 8), 0)
            total = total + jnp.where(chosen > 0.0, block[...].astype(jnp.float32), 0.0)
        out_ref[d] = total.astype(jnp.bfloat16)


def local(
    queries,
    documents,
    doc_len,
    route,
    pair_list,
    attn_gain,
    w_query,
    w_key,
    w_value,
    w_output,
    ffn_gain,
    w_in,
    w_down,
):
    owners = lax.axis_size("pair")
    slices = lax.axis_size("tensor")
    doc_count, doc_rows, width = documents.shape
    query_count, query_rows, _ = queries.shape
    assert query_count * query_rows == doc_rows
    pairs = pair_list.shape[0]
    slots = min(2 * pairs, owners)
    direct = slots == owners
    down_bits = [1 << i for i in range(slices.bit_length() - 1)]
    up_bits = down_bits[::-1]
    attn_gain, ffn_gain = attn_gain.reshape(1, width), ffn_gain.reshape(1, width)
    weights = (w_query, w_key, w_value)

    meta, early, *arrived = kernel_call(
        functools.partial(start_kernel, slots),
        "start",
        (route, doc_len, pair_list, documents, queries),
        [jax.ShapeDtypeStruct((pairs + 1, max(6, owners)), jnp.int32), bf16(1 + direct, 1, doc_rows, width)]
        + [bf16(doc_rows, width)] * owners,
        scratch=[
            pltpu.SMEM(route.shape, jnp.int32),
            pltpu.SMEM(doc_len.shape, jnp.int32),
            pltpu.SMEM(pair_list.shape, jnp.int32),
            pltpu.VMEM(documents.shape, jnp.bfloat16),
            pltpu.VMEM(queries.shape, jnp.bfloat16),
            pltpu.SemaphoreType.DMA((5,)),
        ],
        hbm=(0, 1, 2, 3, 4),
        out_smem=(0,),
        limit=63,
        flops=WAIT,
    )
    arrived = [block if k == 0 else swap(block, k, "pair") for k, block in enumerate(arrived)]
    if not direct:
        me = lax.axis_index("pair")
        taken = lax.dynamic_slice_in_dim(route, me, 1, 1)[:, 0] >= 0
        source = me ^ jnp.arange(owners, dtype=jnp.int32)
        other = jnp.arange(owners, dtype=jnp.int32)
        slot_of = jnp.sum(jnp.where((other[None, :] < source[:, None]) & taken[None, :], 1, 0), 1)
        is_taken = jnp.sum(jnp.where((other[None, :] == source[:, None]) & taken[None, :], 1, 0), 1)
        place = jnp.where(is_taken > 0, slot_of, -1)
        table = (other[:slots, None] == place[None, :]).astype(jnp.bfloat16)
        packed = jnp.einsum("sk,krd->srd", table, jnp.stack(arrived), preferred_element_type=jnp.float32)
        arrived = [packed[s].astype(jnp.bfloat16) for s in range(slots)]
    def spread(kept):
        return kept, swap(kept, up_bits[-1], "tensor")

    top = up_bits[0]
    early = join(early, swap(early, top, "tensor"))
    late = kernel_call(
        stack_kernel, "stack", arrived[direct:], [bf16(slots - direct, 1, doc_rows, width)], flops=WAIT
    )[0]
    late, early = tie(late, early)
    early = gather_blocks(early, up_bits[1:-1])
    first = project("project_early", 1, *spread(early), attn_gain, weights, ())
    late = gather_blocks(join(late, swap(late, top, "tensor")), up_bits[1:-1])
    late, first = tie(late, first)
    late, late_other = spread(late)
    half_done = project_part("project_kept", late, attn_gain, weights)
    q, k, v = project_part(
        "project_came", late_other, attn_gain, weights, tuple(half_done), tuple(first if direct else first[1:])
    )

    groups = [1] * pairs
    swapped = [len(groups) > 1 and g == len(groups) - 1 for g in range(len(groups))]
    part, rest, mine, roles, valid, homes = attend(
        groups, swapped, up_bits, query_rows, doc_count, owners, meta, q, k, v, w_output, late, early if direct else None
    )
    parts = [part]
    if groups[1:]:
        parts += kernel_call(
            functools.partial(output_kernel, groups[1:], swapped[1:]),
            "output",
            (rest, w_output),
            [bf16(2 * n, *part.shape[1:]) for n in groups[1:]],
            flops=2 * rest.size * width,
            moved=2 * w_output.size,
        )
    hidden, pieces = [], []
    for group, part in enumerate(parts):
        order = down_bits[:1] + (down_bits[:0:-1] if swapped[group] else down_bits[1:])
        for bit in order[:-1]:
            kept, came = halve(part, bit)
            part = kept + came
        came = swap(part, order[-1], "tensor")
        own, ffn = settle(sum(groups[:group]), part, came, mine, ffn_gain)
        hidden.append(own)
        pieces += spread(gather_blocks(ffn, order[1:-1][::-1]))
    units = expand(meta, swapped, pieces[::2], w_in, slots)
    units = expand(meta, swapped, pieces[1::2], w_in, slots, tuple(units))[0]
    hidden = jnp.concatenate(hidden, 0)

    columns = 2
    step = width // columns
    pieces = []
    for c in range(columns):
        part = shrink(c * step, step, units, w_down, slices)
        for bit in down_bits:
            kept, came = halve(part, bit)
            if bit != down_bits[-1]:
                part = kept + came
        pieces += [kept, came]
    blocks = kernel_call(
        functools.partial(finish_kernel, 0, columns),
        "finish",
        (roles, valid, hidden, *pieces),
        [bf16(doc_rows, width)] * slots,
    )
    if not direct:
        packed = jnp.einsum("sk,srd->krd", table, jnp.stack(blocks), preferred_element_type=jnp.float32)
        blocks = [packed[s].astype(jnp.bfloat16) for s in range(owners)]
    blocks = [block if k == 0 else swap(block, k, "pair") for k, block in enumerate(blocks)]
    return kernel_call(home_kernel, "home", (homes, *blocks), [bf16(doc_count, doc_rows, width)])[0]


def solution(mesh):
    placed = (
        P("pair", "tensor", None),
        P("pair", "tensor", None),
        P(),
        P(),
        P("pair", None),
        P(),
        P(None, "tensor"),
        P(None, "tensor"),
        P(None, "tensor"),
        P("tensor", None),
        P(),
        P(None, "tensor"),
        P("tensor", None),
    )
    return jax.shard_map(
        local, mesh=mesh, in_specs=placed, out_specs=P("pair", "tensor", None), check_vma=False
    )
```

```python
import functools
import math

import jax
import jax.numpy as jnp
from jax import lax
from jax.experimental import pallas as pl
from jax.experimental.pallas import tpu as pltpu
from jax.sharding import PartitionSpec as P

HEAD = 128
MIB = 1024 * 1024
WAIT = 8 * 10**9


def rms_norm(values, gain):
    spread = jnp.mean(values * values, -1, keepdims=True)
    return values * lax.rsqrt(spread + 1e-06) * gain


def swap(values, bit, axis):
    count = lax.axis_size(axis)
    return lax.ppermute(values, axis, [(i, i ^ bit) for i in range(count)])


def gather_blocks(values, bits):
    for bit in bits:
        values = jnp.concatenate([values, swap(values, bit, "tensor")], 1)
    return values


def halve(values, bit):
    half = values.shape[1] // 2
    return values[:, :half], swap(values[:, half:], bit, "tensor")


def tie(first, second):
    return lax.optimization_barrier((first, second))


def ignoring(kernel, at, count, *refs):
    return kernel(*refs[:at], *refs[at + count :])


def kernel_call(
    kernel, name, operands, out_shape, scratch=(), smem=(), out_smem=(), hbm=(), limit=16, flops=0, moved=0, exps=0, after=()
):
    if after:
        kernel = functools.partial(ignoring, kernel, len(operands), len(after))
    anywhere = [pl.BlockSpec(memory_space=pl.ANY)] * len(after)
    space = lambda yes, far=False: pl.BlockSpec(
        memory_space=pltpu.HBM if far else pltpu.SMEM if yes else pltpu.VMEM
    )
    return pl.pallas_call(
        kernel,
        out_shape=out_shape,
        in_specs=[space(i in smem, i in hbm) for i in range(len(operands))] + anywhere,
        out_specs=[space(i in out_smem) for i in range(len(out_shape))],
        scratch_shapes=list(scratch),
        compiler_params=pltpu.CompilerParams(vmem_limit_bytes=limit * MIB),
        cost_estimate=pl.CostEstimate(flops=flops, bytes_accessed=moved, transcendentals=exps),
        name=name,
    )(*operands, *after)


def bf16(*shape):
    return jax.ShapeDtypeStruct(shape, jnp.bfloat16)


def start_kernel(slots, route_hbm, len_hbm, list_hbm, docs_hbm, queries_hbm, meta_ref, early_ref, *refs):
    route_ref, len_ref, list_ref, docs_ref, queries_ref, sems = refs[-6:]
    send_refs = refs[:-6]
    pieces = (
        (route_hbm, route_ref),
        (docs_hbm, docs_ref),
        (queries_hbm, queries_ref),
        (len_hbm, len_ref),
        (list_hbm, list_ref),
    )
    copies = [pltpu.make_async_copy(a, b, sems.at[i]) for i, (a, b) in enumerate(pieces)]
    for copy in copies:
        copy.start()
    owners = route_ref.shape[0]
    doc_count, doc_rows, width = docs_ref.shape
    me = lax.axis_index("pair")
    copies[0].wait()
    copies[1].wait()
    for k in range(owners):
        picked = docs_ref[jnp.maximum(route_ref[me, me ^ k], 0)]
        send_refs[k][...] = picked
        if k == 0 and slots == owners:
            early_ref[1, 0] = picked
    copies[2].wait()
    asked = queries_ref[...].astype(jnp.float32).reshape(doc_rows, width)
    early_ref[0, 0] = asked.astype(jnp.bfloat16)
    copies[3].wait()
    copies[4].wait()
    for p in range(list_ref.shape[0]):
        meta_ref[p, 0] = list_ref[p, 0]
        for role in range(2):
            source = list_ref[p, 1 + role]
            if slots == owners:
                slot = source ^ me
            else:
                slot = jnp.int32(0)
                for j in range(owners):
                    slot = slot + jnp.where((j < source) & (route_ref[j, me] >= 0), 1, 0)
            meta_ref[p, 1 + role] = slot
            meta_ref[p, 3 + role] = len_ref[source * doc_count + jnp.maximum(route_ref[source, me], 0)]
        meta_ref[p, 5] = lax.axis_index("tensor")
    for k in range(owners):
        meta_ref[list_ref.shape[0], k] = route_ref[me, me ^ k]


def normed(values, gain):
    return rms_norm(values.astype(jnp.float32), gain).astype(jnp.bfloat16)


def stack_kernel(*refs):
    for i, ref in enumerate(refs[:-1]):
        refs[-1][i, 0] = ref[...]


def join_kernel(kept_ref, came_ref, out_ref):
    out_ref[:, :1] = kept_ref[...]
    out_ref[:, 1:] = came_ref[...]


def join(kept, came):
    slots, _, rows, width = kept.shape
    return kernel_call(join_kernel, "join", (kept, came), [bf16(slots, 2, rows, width)], flops=WAIT)[0]


def project_kernel(lead, kept_ref, came_ref, gain_ref, wq_ref, wk_ref, wv_ref, *refs):
    old, (q_ref, k_ref, v_ref) = refs[: len(refs) - 3], refs[len(refs) - 3 :]
    slots, half, rows, width = kept_ref.shape
    group = half * rows
    tall = slots * group
    tokens = jnp.concatenate([kept_ref[...].reshape(tall, width), came_ref[...].reshape(tall, width)], 0)
    tokens = normed(tokens, gain_ref[...])
    scale = math.log2(math.e) / math.sqrt(HEAD)
    base_q, base_kv = 0, 0
    if old:
        base_q, base_kv = old[0].shape[0] if len(old) == 3 else 0, old[-1].shape[0]
        for ref, new_ref in zip(old, (q_ref, k_ref, v_ref)[3 - len(old) :]):
            new_ref[: ref.shape[0]] = ref[...]

    def store(ref, values, first, base):
        count = slots - first
        for part in range(2):
            for s in range(count):
                begin = part * count * group + s * group
                ref[base + s, part * half : (part + 1) * half] = (
                    values[begin : begin + group].astype(jnp.bfloat16).reshape(half, rows, values.shape[1])
                )

    if lead == slots:
        q_ref[...] = jnp.zeros_like(q_ref)
    else:
        asking = tokens
        if lead:
            asking = jnp.concatenate([tokens[lead * group : tall], tokens[tall + lead * group :]], 0)
        store(q_ref, jnp.dot(asking, wq_ref[...], preferred_element_type=jnp.float32) * scale, lead, base_q)
    store(k_ref, jnp.dot(tokens, wk_ref[...], preferred_element_type=jnp.float32), 0, base_kv)
    store(v_ref, jnp.dot(tokens, wv_ref[...], preferred_element_type=jnp.float32), 0, base_kv)


def project(name, lead, kept, came, gain, weights, old):
    slots, half, rows, width = kept.shape
    wide = weights[0].shape[1]
    have_q = old[0].shape[0] if len(old) == 3 else 0
    have_kv = old[-1].shape[0] if old else 0
    nq, nkv = max(have_q + slots - lead, 1), have_kv + slots
    shape = lambda n: bf16(n, 2 * half, rows, wide)
    return kernel_call(
        functools.partial(project_kernel, lead),
        name,
        (kept, came, gain, *weights, *old),
        [shape(nq), shape(nkv), shape(nkv)],
        limit=32,
        flops=2 * 2 * half * rows * width * wide * (3 * slots - lead),
        moved=6 * width * wide,
    )


def project_part_kernel(scale, rows_ref, gain_ref, wq_ref, wk_ref, wv_ref, *refs):
    olds, outs = refs[:-3], refs[-3:]
    slots, half, rows, width = rows_ref.shape
    tokens = normed(rows_ref[...].reshape(slots * half * rows, width), gain_ref[...])
    kept, ahead = olds[:3], (None,) * (6 - len(olds)) + olds[3:] if olds else ()
    for i, (w_ref, out_ref) in enumerate(zip((wq_ref, wk_ref, wv_ref), outs)):
        values = jnp.dot(tokens, w_ref[...], preferred_element_type=jnp.float32)
        if i == 0:
            values = values * scale
        values = values.astype(jnp.bfloat16).reshape(slots, half, rows, values.shape[1])
        if not olds:
            out_ref[...] = values
            continue
        base = out_ref.shape[0] - slots
        if base:
            out_ref[:base] = ahead[i][...]
        out_ref[base:, :half] = kept[i][...]
        out_ref[base:, half:] = values


def project_part(name, rows_in, gain, weights, kept=(), ahead=()):
    slots, half, rows, width = rows_in.shape
    wide = weights[0].shape[1]
    bases = (0,) * (3 - len(ahead)) + tuple(a.shape[0] for a in ahead)
    return kernel_call(
        functools.partial(project_part_kernel, math.log2(math.e) / math.sqrt(HEAD)),
        name,
        (rows_in, gain, *weights, *kept, *ahead),
        [bf16(base + slots, half * (2 if kept else 1), rows, wide) for base in bases],
        limit=24,
        flops=6 * slots * half * rows * width * wide,
        moved=6 * width * wide,
    )


def attend_kernel(bits, query_rows, owners, others, direct, meta, q_ref, k_ref, v_ref, wo_ref, late_ref, *refs):
    early_ref, refs = (refs[0], refs[1:]) if direct else (None, refs)
    out_ref, rest_ref, mine_ref, role_ref, valid_ref, home_ref, ctx_ref, expo_ref = refs
    _, blocks, rows, width = q_ref.shape
    pairs = meta.shape[0] - 1
    slots = valid_ref.shape[0]
    flag = lambda yes: jnp.full((8, 128), yes.astype(jnp.float32), jnp.float32)
    place = lax.broadcasted_iota(jnp.int32, (rows, 128), 0) + meta[0, 5] * rows
    lengths = [jnp.int32(0)] * slots
    for p in range(pairs):
        for role in range(2):
            slot = meta[p, 1 + role]
            for part, at in enumerate((0, others[p])):
                if direct:
                    chosen = late_ref[jnp.maximum(slot - 1, 0), at]
                    mine_ref[p, role, part] = jnp.where(slot == 0, early_ref[1, at], chosen)
                else:
                    mine_ref[p, role, part] = late_ref[slot, at]
            for s in range(slots):
                role_ref[2 * p + role, s] = flag(slot == s)
                lengths[s] = jnp.where(slot == s, meta[p, 3 + role], lengths[s])
    for s in range(slots):
        valid_ref[s] = (place < lengths[s]).astype(jnp.float32)
    for d in range(home_ref.shape[0]):
        for k in range(owners):
            home_ref[d, k] = flag(meta[pairs, k] == d)
    keys = blocks * rows
    heads = width // HEAD
    lane = lax.broadcasted_iota(jnp.int32, (1, keys), 1)
    block, row = lane // rows, lane % rows
    origin = jnp.zeros_like(lane)
    for place, bit in enumerate(bits):
        origin = origin + ((block >> place) & 1) * bit
    position = (origin ^ meta[0, 5]) * rows + row
    keep = lambda yes: jnp.where(yes, 0.0, jnp.float32(-1e30))
    ones = jnp.ones((3 * keys, HEAD), jnp.bfloat16)

    def rows_of(ref, places, at):
        return jnp.concatenate([ref[place, :, :, at].reshape(keys, HEAD) for place in places], 0)

    def one_pair(pair, carry):
        query, first, second = meta[pair, 0], meta[pair, 1], meta[pair, 2]
        bias = jnp.concatenate(
            [
                keep(position < meta[pair, 3]),
                keep(position < meta[pair, 4]),
                keep((row >= query * query_rows) & (row < (query + 1) * query_rows)),
            ],
            1,
        )
        def weigh(head):
            at = slice(head * HEAD, (head + 1) * HEAD)
            qs = rows_of(q_ref, (first, second), at)
            ks = rows_of(k_ref, (first + 1, second + 1, 0), at)
            scores = lax.dot_general(qs, ks, (((1,), (1,)), ((), ())), preferred_element_type=jnp.float32) + bias
            top = jnp.max(scores, -1, keepdims=True)
            expo_ref[head] = jnp.exp2(scores - top).astype(jnp.bfloat16)

        def mix(head):
            at = slice(head * HEAD, (head + 1) * HEAD)
            vs = rows_of(v_ref, (first + 1, second + 1, 0), at)
            mixed = jnp.dot(expo_ref[head], jnp.concatenate([vs, ones], 1), preferred_element_type=jnp.float32)
            ctx_ref[pl.ds(pl.multiple_of(pair * 2 * keys, 2 * keys), 2 * keys), at] = (
                mixed[:, :HEAD] / mixed[:, HEAD:]
            ).astype(jnp.bfloat16)

        ahead = min(3, heads)
        for head in range(heads + ahead):
            if head < heads:
                weigh(head)
            if head >= ahead:
                mix(head - ahead)
        return carry

    lax.fori_loop(0, pairs, one_pair, 0, unroll=True)
    begin = out_ref.shape[0] * keys
    product = jnp.dot(ctx_ref[:begin], wo_ref[...], preferred_element_type=jnp.float32)
    out_ref[...] = product.astype(jnp.bfloat16).reshape(out_ref.shape)
    if begin < ctx_ref.shape[0]:
        rest_ref[...] = ctx_ref[begin:]


def attend(groups, swapped, bits, query_rows, doc_count, owners, meta, q, k, v, w_output, late, early):
    _, blocks, rows, width = q.shape
    pairs, model, slots, lead = meta.shape[0] - 1, w_output.shape[1], q.shape[0], groups[0]
    others = [late.shape[1] // 2 if far else 1 for n, far in zip(groups, swapped) for _ in range(n)]
    f32 = lambda *shape: jax.ShapeDtypeStruct(shape, jnp.float32)
    tall = 2 * blocks * rows
    return kernel_call(
        functools.partial(attend_kernel, bits, query_rows, owners, others, early is not None),
        "attend",
        (meta, q, k, v, w_output, late) + (() if early is None else (early,)),
        [
            bf16(2 * lead, blocks, rows, model),
            bf16(max(pairs - lead, 1) * tall, width),
            bf16(pairs, 2, 2, *late.shape[2:]),
            f32(2 * pairs, slots, 8, 128),
            f32(slots, rows, 128),
            f32(doc_count, owners, 8, 128),
        ],
        scratch=[
            pltpu.VMEM((pairs * tall, width), jnp.bfloat16),
            pltpu.VMEM((width // HEAD, tall, tall * 3 // 2), jnp.bfloat16),
        ],
        smem=(0,),
        flops=2 * tall * width * (model + 3 * pairs * tall),
        moved=2 * model * width,
        exps=pairs * width // HEAD * tall * tall * 3 // 2,
    )


def turned(blocks):
    bits = blocks.bit_length() - 1
    return [sum(((b >> i) & 1) << (bits - 1 - i) for i in range(bits)) for b in range(blocks)]


def output_kernel(groups, swapped, ctx_ref, wo_ref, *out_refs):
    product = jnp.dot(ctx_ref[...], wo_ref[...], preferred_element_type=jnp.float32).astype(jnp.bfloat16)
    tall = ctx_ref.shape[0] // sum(groups)
    for i, out_ref in enumerate(out_refs):
        begin = sum(groups[:i])
        values = product[begin * tall : (begin + groups[i]) * tall].reshape(out_ref.shape)
        if not swapped[i]:
            out_ref[...] = values
            continue
        half = out_ref.shape[1] // 2
        for b, to in enumerate(turned(half)):
            out_ref[:, to] = values[:, b]
            out_ref[:, half + to] = values[:, half + b]


def settle_kernel(pair, kept_ref, came_ref, mine_ref, gain_ref, hidden_ref, ffn_ref):
    for role in range(kept_ref.shape[0]):
        for part in range(2):
            summed = kept_ref[role, part].astype(jnp.float32) + came_ref[role, 1 - part].astype(jnp.float32)
            hidden = mine_ref[pair + role // 2, role % 2, part].astype(jnp.float32) + summed
            if part == 0:
                hidden_ref[role] = hidden
            ffn_ref[role, part] = rms_norm(hidden, gain_ref[...]).astype(jnp.bfloat16)


def settle(pair, kept, came, mine, gain):
    roles, _, count, width = kept.shape
    return kernel_call(
        functools.partial(settle_kernel, pair),
        "settle",
        (kept, came, mine, gain),
        [jax.ShapeDtypeStruct((roles, count, width), jnp.float32), bf16(roles, 2, count, width)],
    )


def expand_kernel(swapped, tile, meta, w_ref, *refs):
    pieces, rest = refs[: len(swapped)], refs[len(swapped) :]
    old_ref, out_ref = (rest[0] if len(rest) == 2 else None), rest[-1]
    _, half, rows, width = pieces[0].shape
    group = half * rows
    tokens = []
    for piece, far in zip(pieces, swapped):
        for r in range(piece.shape[0]):
            if far:
                tokens += [piece[r, b] for b in turned(half)]
            else:
                tokens.append(piece[r].reshape(group, width))
    tokens = jnp.concatenate(tokens, 0)
    last = out_ref.shape[0] - 1

    def step(i, carry):
        at = pl.ds(pl.multiple_of(i * tile, tile), tile)
        units = jnp.maximum(jnp.dot(tokens, w_ref[:, at], preferred_element_type=jnp.float32), 0.0)
        units = units.astype(jnp.bfloat16)
        if old_ref is not None:
            out_ref[0, :, :, at] = old_ref[0, :, :, at]
        out_ref[last, :, :, at] = jnp.zeros((out_ref.shape[1], group, tile), jnp.bfloat16)
        for r in range(tokens.shape[0] // group):
            slot = meta[r // 2, 1 + r % 2]
            out_ref[last, slot, :, at] = out_ref[last, slot, :, at] + units[r * group : (r + 1) * group]
        return carry

    lax.fori_loop(0, w_ref.shape[1] // tile, step, 0, unroll=4)


def expand(meta, swapped, pieces, w_in, slots, old=()):
    _, half, rows, width = pieces[0].shape
    units = w_in.shape[1]
    roles = sum(piece.shape[0] for piece in pieces)
    return kernel_call(
        functools.partial(expand_kernel, swapped, min(512, units)),
        "expand",
        (meta, w_in, *pieces, *old),
        [bf16(1 + len(old), slots, half * rows, units)],
        smem=(0,),
        limit=24,
        flops=2 * roles * half * rows * width * units,
        moved=2 * width * units,
    )


def shrink_kernel(begin, units_ref, w_ref, out_ref):
    parts, slots, tall, depth = units_ref.shape
    _, blocks, rows, step = out_ref.shape
    product = jnp.dot(
        units_ref[...].reshape(parts * slots * tall, depth),
        w_ref[:, begin : begin + step],
        preferred_element_type=jnp.float32,
    )
    product = product.astype(jnp.bfloat16).reshape(parts, slots, blocks // parts, rows, step)
    for part in range(parts):
        out_ref[:, part * (blocks // parts) : (part + 1) * (blocks // parts)] = product[part]


def shrink(begin, step, units, w_down, blocks):
    parts, slots, tall, depth = units.shape
    return kernel_call(
        functools.partial(shrink_kernel, begin),
        "shrink",
        (units, w_down),
        [bf16(slots, blocks, parts * tall // blocks, step)],
        limit=24,
        flops=2 * parts * slots * tall * depth * step,
        moved=2 * depth * step,
    )[0]


def wide(flags, width):
    return jnp.concatenate([flags] * (width // 128), 1)


def finish_kernel(low, columns, role_ref, valid_ref, hidden_ref, *refs):
    pieces, out_refs = refs[: 2 * columns], refs[2 * columns :]
    roles, rows, width = hidden_ref.shape
    for i, out_ref in enumerate(out_refs):
        total = jnp.concatenate(
            [
                pieces[2 * c][i, 0].astype(jnp.float32) + pieces[2 * c + 1][i, 0].astype(jnp.float32)
                for c in range(columns)
            ],
            1,
        )
        for r in range(roles):
            chosen = jnp.concatenate([wide(role_ref[r, low + i], width)] * (rows // 8), 0)
            total = total + jnp.where(chosen > 0.0, hidden_ref[r], 0.0)
        valid = wide(valid_ref[low + i], width) > 0.0
        out_ref[...] = jnp.where(valid, total, 0.0).astype(jnp.bfloat16)


def home_kernel(home_ref, *refs):
    blocks, out_ref = refs[:-1], refs[-1]
    rows, width = blocks[0].shape
    for d in range(out_ref.shape[0]):
        total = jnp.zeros((rows, width), jnp.float32)
        for k, block in enumerate(blocks):
            chosen = jnp.concatenate([wide(home_ref[d, k], width)] * (rows // 8), 0)
            total = total + jnp.where(chosen > 0.0, block[...].astype(jnp.float32), 0.0)
        out_ref[d] = total.astype(jnp.bfloat16)


def local(
    queries,
    documents,
    doc_len,
    route,
    pair_list,
    attn_gain,
    w_query,
    w_key,
    w_value,
    w_output,
    ffn_gain,
    w_in,
    w_down,
):
    owners = lax.axis_size("pair")
    slices = lax.axis_size("tensor")
    doc_count, doc_rows, width = documents.shape
    query_count, query_rows, _ = queries.shape
    assert query_count * query_rows == doc_rows
    pairs = pair_list.shape[0]
    slots = min(2 * pairs, owners)
    direct = slots == owners
    down_bits = [1 << i for i in range(slices.bit_length() - 1)]
    up_bits = down_bits[::-1]
    attn_gain, ffn_gain = attn_gain.reshape(1, width), ffn_gain.reshape(1, width)
    weights = (w_query, w_key, w_value)

    meta, early, *arrived = kernel_call(
        functools.partial(start_kernel, slots),
        "start",
        (route, doc_len, pair_list, documents, queries),
        [jax.ShapeDtypeStruct((pairs + 1, max(6, owners)), jnp.int32), bf16(1 + direct, 1, doc_rows, width)]
        + [bf16(doc_rows, width)] * owners,
        scratch=[
            pltpu.SMEM(route.shape, jnp.int32),
            pltpu.SMEM(doc_len.shape, jnp.int32),
            pltpu.SMEM(pair_list.shape, jnp.int32),
            pltpu.VMEM(documents.shape, jnp.bfloat16),
            pltpu.VMEM(queries.shape, jnp.bfloat16),
            pltpu.SemaphoreType.DMA((5,)),
        ],
        hbm=(0, 1, 2, 3, 4),
        out_smem=(0,),
        limit=63,
        flops=WAIT,
    )
    arrived = [block if k == 0 else swap(block, k, "pair") for k, block in enumerate(arrived)]
    if not direct:
        me = lax.axis_index("pair")
        taken = lax.dynamic_slice_in_dim(route, me, 1, 1)[:, 0] >= 0
        source = me ^ jnp.arange(owners, dtype=jnp.int32)
        other = jnp.arange(owners, dtype=jnp.int32)
        slot_of = jnp.sum(jnp.where((other[None, :] < source[:, None]) & taken[None, :], 1, 0), 1)
        is_taken = jnp.sum(jnp.where((other[None, :] == source[:, None]) & taken[None, :], 1, 0), 1)
        place = jnp.where(is_taken > 0, slot_of, -1)
        table = (other[:slots, None] == place[None, :]).astype(jnp.bfloat16)
        packed = jnp.einsum("sk,krd->srd", table, jnp.stack(arrived), preferred_element_type=jnp.float32)
        arrived = [packed[s].astype(jnp.bfloat16) for s in range(slots)]
    def spread(kept):
        return kept, swap(kept, up_bits[-1], "tensor")

    top = up_bits[0]
    early = join(early, swap(early, top, "tensor"))
    late = kernel_call(
        stack_kernel, "stack", arrived[direct:], [bf16(slots - direct, 1, doc_rows, width)], flops=WAIT
    )[0]
    late, early = tie(late, early)
    early = gather_blocks(early, up_bits[1:-1])
    first = project("project_early", 1, *spread(early), attn_gain, weights, ())
    late = gather_blocks(join(late, swap(late, top, "tensor")), up_bits[1:-1])
    late, first = tie(late, first)
    late, late_other = spread(late)
    half_done = project_part("project_kept", late, attn_gain, weights)
    q, k, v = project_part(
        "project_came", late_other, attn_gain, weights, tuple(half_done), tuple(first if direct else first[1:])
    )

    groups = [1] * pairs
    swapped = [len(groups) > 1 and g == len(groups) - 1 for g in range(len(groups))]
    part, rest, mine, roles, valid, homes = attend(
        groups, swapped, up_bits, query_rows, doc_count, owners, meta, q, k, v, w_output, late, early if direct else None
    )
    parts = [part]
    if groups[1:]:
        parts += kernel_call(
            functools.partial(output_kernel, groups[1:], swapped[1:]),
            "output",
            (rest, w_output),
            [bf16(2 * n, *part.shape[1:]) for n in groups[1:]],
            flops=2 * rest.size * width,
            moved=2 * w_output.size,
        )
    hidden, pieces = [], []
    for group, part in enumerate(parts):
        order = down_bits[:1] + (down_bits[:0:-1] if swapped[group] else down_bits[1:])
        for bit in order[:-1]:
            kept, came = halve(part, bit)
            part = kept + came
        came = swap(part, order[-1], "tensor")
        own, ffn = settle(sum(groups[:group]), part, came, mine, ffn_gain)
        hidden.append(own)
        pieces += spread(gather_blocks(ffn, order[1:-1][::-1]))
    units = expand(meta, swapped, pieces[::2], w_in, slots)
    units = expand(meta, swapped, pieces[1::2], w_in, slots, tuple(units))[0]
    hidden = jnp.concatenate(hidden, 0)

    columns = 2
    step = width // columns
    pieces = []
    for c in range(columns):
        part = shrink(c * step, step, units, w_down, slices)
        for bit in down_bits:
            kept, came = halve(part, bit)
            if bit != down_bits[-1]:
                part = kept + came
        pieces += [kept, came]
    blocks = kernel_call(
        functools.partial(finish_kernel, 0, columns),
        "finish",
        (roles, valid, hidden, *pieces),
        [bf16(doc_rows, width)] * slots,
    )
    if not direct:
        packed = jnp.einsum("sk,srd->krd", table, jnp.stack(blocks), preferred_element_type=jnp.float32)
        blocks = [packed[s].astype(jnp.bfloat16) for s in range(owners)]
    blocks = [block if k == 0 else swap(block, k, "pair") for k, block in enumerate(blocks)]
    return kernel_call(home_kernel, "home", (homes, *blocks), [bf16(doc_count, doc_rows, width)])[0]


def solution(mesh):
    placed = (
        P("pair", "tensor", None),
        P("pair", "tensor", None),
        P(),
        P(),
        P("pair", None),
        P(),
        P(None, "tensor"),
        P(None, "tensor"),
        P(None, "tensor"),
        P("tensor", None),
        P(),
        P(None, "tensor"),
        P("tensor", None),
    )
    return jax.shard_map(
        local, mesh=mesh, in_specs=placed, out_specs=P("pair", "tensor", None), check_vma=False
    )
```

```python
import functools
import math

import jax
import jax.numpy as jnp
from jax import lax
from jax.experimental import pallas as pl
from jax.experimental.pallas import tpu as pltpu
from jax.sharding import PartitionSpec as P

HEAD = 128
MIB = 1024 * 1024
WAIT = 8 * 10**9


def rms_norm(values, gain):
    spread = jnp.mean(values * values, -1, keepdims=True)
    return values * lax.rsqrt(spread + 1e-06) * gain


def swap(values, bit, axis):
    count = lax.axis_size(axis)
    return lax.ppermute(values, axis, [(i, i ^ bit) for i in range(count)])


def gather_blocks(values, bits):
    for bit in bits:
        values = jnp.concatenate([values, swap(values, bit, "tensor")], 1)
    return values


def halve(values, bit):
    half = values.shape[1] // 2
    return values[:, :half], swap(values[:, half:], bit, "tensor")


def tie(first, second):
    return lax.optimization_barrier((first, second))


def ignoring(kernel, at, count, *refs):
    return kernel(*refs[:at], *refs[at + count :])


def kernel_call(
    kernel, name, operands, out_shape, scratch=(), smem=(), out_smem=(), hbm=(), limit=16, flops=0, moved=0, exps=0, after=()
):
    if after:
        kernel = functools.partial(ignoring, kernel, len(operands), len(after))
    anywhere = [pl.BlockSpec(memory_space=pl.ANY)] * len(after)
    space = lambda yes, far=False: pl.BlockSpec(
        memory_space=pltpu.HBM if far else pltpu.SMEM if yes else pltpu.VMEM
    )
    return pl.pallas_call(
        kernel,
        out_shape=out_shape,
        in_specs=[space(i in smem, i in hbm) for i in range(len(operands))] + anywhere,
        out_specs=[space(i in out_smem) for i in range(len(out_shape))],
        scratch_shapes=list(scratch),
        compiler_params=pltpu.CompilerParams(vmem_limit_bytes=limit * MIB),
        cost_estimate=pl.CostEstimate(flops=flops, bytes_accessed=moved, transcendentals=exps),
        name=name,
    )(*operands, *after)


def bf16(*shape):
    return jax.ShapeDtypeStruct(shape, jnp.bfloat16)


def start_kernel(slots, route_hbm, len_hbm, list_hbm, docs_hbm, queries_hbm, meta_ref, early_ref, *refs):
    route_ref, len_ref, list_ref, docs_ref, queries_ref, sems = refs[-6:]
    send_refs = refs[:-6]
    pieces = (
        (route_hbm, route_ref),
        (docs_hbm, docs_ref),
        (queries_hbm, queries_ref),
        (len_hbm, len_ref),
        (list_hbm, list_ref),
    )
    copies = [pltpu.make_async_copy(a, b, sems.at[i]) for i, (a, b) in enumerate(pieces)]
    for copy in copies:
        copy.start()
    owners = route_ref.shape[0]
    doc_count, doc_rows, width = docs_ref.shape
    me = lax.axis_index("pair")
    copies[0].wait()
    copies[1].wait()
    for k in range(owners):
        picked = docs_ref[jnp.maximum(route_ref[me, me ^ k], 0)]
        send_refs[k][...] = picked
        if k == 0 and slots == owners:
            early_ref[1, 0] = picked
    copies[2].wait()
    asked = queries_ref[...].astype(jnp.float32).reshape(doc_rows, width)
    early_ref[0, 0] = asked.astype(jnp.bfloat16)
    copies[3].wait()
    copies[4].wait()
    for p in range(list_ref.shape[0]):
        meta_ref[p, 0] = list_ref[p, 0]
        for role in range(2):
            source = list_ref[p, 1 + role]
            if slots == owners:
                slot = source ^ me
            else:
                slot = jnp.int32(0)
                for j in range(owners):
                    slot = slot + jnp.where((j < source) & (route_ref[j, me] >= 0), 1, 0)
            meta_ref[p, 1 + role] = slot
            meta_ref[p, 3 + role] = len_ref[source * doc_count + jnp.maximum(route_ref[source, me], 0)]
        meta_ref[p, 5] = lax.axis_index("tensor")
    for k in range(owners):
        meta_ref[list_ref.shape[0], k] = route_ref[me, me ^ k]


def normed(values, gain):
    return rms_norm(values.astype(jnp.float32), gain).astype(jnp.bfloat16)


def stack_kernel(*refs):
    for i, ref in enumerate(refs[-2::-1]):
        refs[-1][i, 0] = ref[...]


def join_kernel(kept_ref, came_ref, out_ref):
    out_ref[:, :1] = kept_ref[...]
    out_ref[:, 1:] = came_ref[...]


def join(kept, came):
    slots, _, rows, width = kept.shape
    return kernel_call(join_kernel, "join", (kept, came), [bf16(slots, 2, rows, width)], flops=WAIT)[0]


def project_kernel(lead, kept_ref, came_ref, gain_ref, wq_ref, wk_ref, wv_ref, *refs):
    old, (q_ref, k_ref, v_ref) = refs[: len(refs) - 3], refs[len(refs) - 3 :]
    slots, half, rows, width = kept_ref.shape
    group = half * rows
    tall = slots * group
    tokens = jnp.concatenate([kept_ref[...].reshape(tall, width), came_ref[...].reshape(tall, width)], 0)
    tokens = normed(tokens, gain_ref[...])
    scale = math.log2(math.e) / math.sqrt(HEAD)
    base_q, base_kv = 0, 0
    if old:
        base_q, base_kv = old[0].shape[0] if len(old) == 3 else 0, old[-1].shape[0]
        for ref, new_ref in zip(old, (q_ref, k_ref, v_ref)[3 - len(old) :]):
            new_ref[: ref.shape[0]] = ref[...]

    def store(ref, values, first, base):
        count = slots - first
        for part in range(2):
            for s in range(count):
                begin = part * count * group + s * group
                ref[base + s, part * half : (part + 1) * half] = (
                    values[begin : begin + group].astype(jnp.bfloat16).reshape(half, rows, values.shape[1])
                )

    if lead == slots:
        q_ref[...] = jnp.zeros_like(q_ref)
    else:
        asking = tokens
        if lead:
            asking = jnp.concatenate([tokens[lead * group : tall], tokens[tall + lead * group :]], 0)
        store(q_ref, jnp.dot(asking, wq_ref[...], preferred_element_type=jnp.float32) * scale, lead, base_q)
    store(k_ref, jnp.dot(tokens, wk_ref[...], preferred_element_type=jnp.float32), 0, base_kv)
    store(v_ref, jnp.dot(tokens, wv_ref[...], preferred_element_type=jnp.float32), 0, base_kv)


def project(name, lead, kept, came, gain, weights, old):
    slots, half, rows, width = kept.shape
    wide = weights[0].shape[1]
    have_q = old[0].shape[0] if len(old) == 3 else 0
    have_kv = old[-1].shape[0] if old else 0
    nq, nkv = max(have_q + slots - lead, 1), have_kv + slots
    shape = lambda n: bf16(n, 2 * half, rows, wide)
    return kernel_call(
        functools.partial(project_kernel, lead),
        name,
        (kept, came, gain, *weights, *old),
        [shape(nq), shape(nkv), shape(nkv)],
        limit=32,
        flops=2 * 2 * half * rows * width * wide * (3 * slots - lead),
        moved=6 * width * wide,
    )


def project_part_kernel(scale, rows_ref, gain_ref, wq_ref, wk_ref, wv_ref, *refs):
    olds, outs = refs[:-3], refs[-3:]
    slots, half, rows, width = rows_ref.shape
    tokens = normed(rows_ref[...].reshape(slots * half * rows, width), gain_ref[...])
    kept, ahead = olds[:3], (None,) * (6 - len(olds)) + olds[3:] if olds else ()
    for i, (w_ref, out_ref) in enumerate(zip((wq_ref, wk_ref, wv_ref), outs)):
        values = jnp.dot(tokens, w_ref[...], preferred_element_type=jnp.float32)
        if i == 0:
            values = values * scale
        values = values.astype(jnp.bfloat16).reshape(slots, half, rows, values.shape[1])
        if not olds:
            out_ref[...] = values
            continue
        base = out_ref.shape[0] - slots
        if base:
            out_ref[:base] = ahead[i][...]
        out_ref[base:, :half] = kept[i][...]
        out_ref[base:, half:] = values


def project_part(name, rows_in, gain, weights, kept=(), ahead=()):
    slots, half, rows, width = rows_in.shape
    wide = weights[0].shape[1]
    bases = (0,) * (3 - len(ahead)) + tuple(a.shape[0] for a in ahead)
    return kernel_call(
        functools.partial(project_part_kernel, math.log2(math.e) / math.sqrt(HEAD)),
        name,
        (rows_in, gain, *weights, *kept, *ahead),
        [bf16(base + slots, half * (2 if kept else 1), rows, wide) for base in bases],
        limit=24,
        flops=6 * slots * half * rows * width * wide,
        moved=6 * width * wide,
    )


def attend_kernel(bits, query_rows, owners, others, direct, meta, q_ref, k_ref, v_ref, wo_ref, late_ref, *refs):
    early_ref, refs = (refs[0], refs[1:]) if direct else (None, refs)
    out_ref, rest_ref, mine_ref, role_ref, valid_ref, home_ref, ctx_ref, expo_ref = refs
    _, blocks, rows, width = q_ref.shape
    pairs = meta.shape[0] - 1
    slots = valid_ref.shape[0]
    flag = lambda yes: jnp.full((8, 128), yes.astype(jnp.float32), jnp.float32)
    place = lax.broadcasted_iota(jnp.int32, (rows, 128), 0) + meta[0, 5] * rows
    lengths = [jnp.int32(0)] * slots
    for p in range(pairs):
        for role in range(2):
            slot = meta[p, 1 + role]
            for part, at in enumerate((0, others[p])):
                if direct:
                    chosen = late_ref[jnp.maximum(slot - 1, 0), at]
                    mine_ref[p, role, part] = jnp.where(slot == 0, early_ref[1, at], chosen)
                else:
                    mine_ref[p, role, part] = late_ref[slot, at]
            for s in range(slots):
                role_ref[2 * p + role, s] = flag(slot == s)
                lengths[s] = jnp.where(slot == s, meta[p, 3 + role], lengths[s])
    for s in range(slots):
        valid_ref[s] = (place < lengths[s]).astype(jnp.float32)
    for d in range(home_ref.shape[0]):
        for k in range(owners):
            home_ref[d, k] = flag(meta[pairs, k] == d)
    keys = blocks * rows
    heads = width // HEAD
    lane = lax.broadcasted_iota(jnp.int32, (1, keys), 1)
    block, row = lane // rows, lane % rows
    origin = jnp.zeros_like(lane)
    for place, bit in enumerate(bits):
        origin = origin + ((block >> place) & 1) * bit
    position = (origin ^ meta[0, 5]) * rows + row
    keep = lambda yes: jnp.where(yes, 0.0, jnp.float32(-1e30))
    ones = jnp.ones((3 * keys, HEAD), jnp.bfloat16)

    def rows_of(ref, places, at):
        return jnp.concatenate([ref[place, :, :, at].reshape(keys, HEAD) for place in places], 0)

    def one_pair(pair, carry):
        query, first, second = meta[pair, 0], meta[pair, 1], meta[pair, 2]
        bias = jnp.concatenate(
            [
                keep(position < meta[pair, 3]),
                keep(position < meta[pair, 4]),
                keep((row >= query * query_rows) & (row < (query + 1) * query_rows)),
            ],
            1,
        )
        def weigh(head):
            at = slice(head * HEAD, (head + 1) * HEAD)
            qs = rows_of(q_ref, (first, second), at)
            ks = rows_of(k_ref, (first + 1, second + 1, 0), at)
            scores = lax.dot_general(qs, ks, (((1,), (1,)), ((), ())), preferred_element_type=jnp.float32) + bias
            top = jnp.max(scores, -1, keepdims=True)
            expo_ref[head] = jnp.exp2(scores - top).astype(jnp.bfloat16)

        def mix(head):
            at = slice(head * HEAD, (head + 1) * HEAD)
            vs = rows_of(v_ref, (first + 1, second + 1, 0), at)
            mixed = jnp.dot(expo_ref[head], jnp.concatenate([vs, ones], 1), preferred_element_type=jnp.float32)
            ctx_ref[pl.ds(pl.multiple_of(pair * 2 * keys, 2 * keys), 2 * keys), at] = (
                mixed[:, :HEAD] / mixed[:, HEAD:]
            ).astype(jnp.bfloat16)

        ahead = min(3, heads)
        for head in range(heads + ahead):
            if head < heads:
                weigh(head)
            if head >= ahead:
                mix(head - ahead)
        return carry

    lax.fori_loop(0, pairs, one_pair, 0, unroll=True)
    begin = out_ref.shape[0] * keys
    product = jnp.dot(ctx_ref[:begin], wo_ref[...], preferred_element_type=jnp.float32)
    out_ref[...] = product.astype(jnp.bfloat16).reshape(out_ref.shape)
    if begin < ctx_ref.shape[0]:
        rest_ref[...] = ctx_ref[begin:]


def attend(groups, swapped, bits, query_rows, doc_count, owners, meta, q, k, v, w_output, late, early):
    _, blocks, rows, width = q.shape
    pairs, model, slots, lead = meta.shape[0] - 1, w_output.shape[1], q.shape[0], groups[0]
    others = [late.shape[1] // 2 if far else 1 for n, far in zip(groups, swapped) for _ in range(n)]
    f32 = lambda *shape: jax.ShapeDtypeStruct(shape, jnp.float32)
    tall = 2 * blocks * rows
    return kernel_call(
        functools.partial(attend_kernel, bits, query_rows, owners, others, early is not None),
        "attend",
        (meta, q, k, v, w_output, late) + (() if early is None else (early,)),
        [
            bf16(2 * lead, blocks, rows, model),
            bf16(max(pairs - lead, 1) * tall, width),
            bf16(pairs, 2, 2, *late.shape[2:]),
            f32(2 * pairs, slots, 8, 128),
            f32(slots, rows, 128),
            f32(doc_count, owners, 8, 128),
        ],
        scratch=[
            pltpu.VMEM((pairs * tall, width), jnp.bfloat16),
            pltpu.VMEM((width // HEAD, tall, tall * 3 // 2), jnp.bfloat16),
        ],
        smem=(0,),
        flops=2 * tall * width * (model + 3 * pairs * tall),
        moved=2 * model * width,
        exps=pairs * width // HEAD * tall * tall * 3 // 2,
    )


def turned(blocks):
    bits = blocks.bit_length() - 1
    return [sum(((b >> i) & 1) << (bits - 1 - i) for i in range(bits)) for b in range(blocks)]


def output_kernel(groups, swapped, ctx_ref, wo_ref, *out_refs):
    product = jnp.dot(ctx_ref[...], wo_ref[...], preferred_element_type=jnp.float32).astype(jnp.bfloat16)
    tall = ctx_ref.shape[0] // sum(groups)
    for i, out_ref in enumerate(out_refs):
        begin = sum(groups[:i])
        values = product[begin * tall : (begin + groups[i]) * tall].reshape(out_ref.shape)
        if not swapped[i]:
            out_ref[...] = values
            continue
        half = out_ref.shape[1] // 2
        for b, to in enumerate(turned(half)):
            out_ref[:, to] = values[:, b]
            out_ref[:, half + to] = values[:, half + b]


def settle_kernel(pair, kept_ref, came_ref, mine_ref, gain_ref, hidden_ref, ffn_ref):
    for role in range(kept_ref.shape[0]):
        for part in range(2):
            summed = kept_ref[role, part].astype(jnp.float32) + came_ref[role, 1 - part].astype(jnp.float32)
            hidden = mine_ref[pair + role // 2, role % 2, part].astype(jnp.float32) + summed
            if part == 0:
                hidden_ref[role] = hidden
            ffn_ref[role, part] = rms_norm(hidden, gain_ref[...]).astype(jnp.bfloat16)


def settle(pair, kept, came, mine, gain):
    roles, _, count, width = kept.shape
    return kernel_call(
        functools.partial(settle_kernel, pair),
        "settle",
        (kept, came, mine, gain),
        [jax.ShapeDtypeStruct((roles, count, width), jnp.float32), bf16(roles, 2, count, width)],
    )


def expand_kernel(swapped, tile, meta, w_ref, *refs):
    pieces, rest = refs[: len(swapped)], refs[len(swapped) :]
    old_ref, out_ref = (rest[0] if len(rest) == 2 else None), rest[-1]
    _, half, rows, width = pieces[0].shape
    group = half * rows
    tokens = []
    for piece, far in zip(pieces, swapped):
        for r in range(piece.shape[0]):
            if far:
                tokens += [piece[r, b] for b in turned(half)]
            else:
                tokens.append(piece[r].reshape(group, width))
    tokens = jnp.concatenate(tokens, 0)
    last = out_ref.shape[0] - 1

    def step(i, carry):
        at = pl.ds(pl.multiple_of(i * tile, tile), tile)
        units = jnp.maximum(jnp.dot(tokens, w_ref[:, at], preferred_element_type=jnp.float32), 0.0)
        units = units.astype(jnp.bfloat16)
        if old_ref is not None:
            out_ref[0, :, :, at] = old_ref[0, :, :, at]
        out_ref[last, :, :, at] = jnp.zeros((out_ref.shape[1], group, tile), jnp.bfloat16)
        for r in range(tokens.shape[0] // group):
            slot = meta[r // 2, 1 + r % 2]
            out_ref[last, slot, :, at] = out_ref[last, slot, :, at] + units[r * group : (r + 1) * group]
        return carry

    lax.fori_loop(0, w_ref.shape[1] // tile, step, 0, unroll=4)


def expand(meta, swapped, pieces, w_in, slots, old=()):
    _, half, rows, width = pieces[0].shape
    units = w_in.shape[1]
    roles = sum(piece.shape[0] for piece in pieces)
    return kernel_call(
        functools.partial(expand_kernel, swapped, min(512, units)),
        "expand",
        (meta, w_in, *pieces, *old),
        [bf16(1 + len(old), slots, half * rows, units)],
        smem=(0,),
        limit=24,
        flops=2 * roles * half * rows * width * units,
        moved=2 * width * units,
    )


def shrink_kernel(begin, units_ref, w_ref, out_ref):
    parts, slots, tall, depth = units_ref.shape
    _, blocks, rows, step = out_ref.shape
    product = jnp.dot(
        units_ref[...].reshape(parts * slots * tall, depth),
        w_ref[:, begin : begin + step],
        preferred_element_type=jnp.float32,
    )
    product = product.astype(jnp.bfloat16).reshape(parts, slots, blocks // parts, rows, step)
    for part in range(parts):
        out_ref[:, part * (blocks // parts) : (part + 1) * (blocks // parts)] = product[part]


def shrink(begin, step, units, w_down, blocks):
    parts, slots, tall, depth = units.shape
    return kernel_call(
        functools.partial(shrink_kernel, begin),
        "shrink",
        (units, w_down),
        [bf16(slots, blocks, parts * tall // blocks, step)],
        limit=24,
        flops=2 * parts * slots * tall * depth * step,
        moved=2 * depth * step,
    )[0]


def wide(flags, width):
    return jnp.concatenate([flags] * (width // 128), 1)


def finish_kernel(low, columns, role_ref, valid_ref, hidden_ref, *refs):
    pieces, out_refs = refs[: 2 * columns], refs[2 * columns :]
    roles, rows, width = hidden_ref.shape
    for i, out_ref in enumerate(out_refs):
        total = jnp.concatenate(
            [
                pieces[2 * c][i, 0].astype(jnp.float32) + pieces[2 * c + 1][i, 0].astype(jnp.float32)
                for c in range(columns)
            ],
            1,
        )
        for r in range(roles):
            chosen = jnp.concatenate([wide(role_ref[r, low + i], width)] * (rows // 8), 0)
            total = total + jnp.where(chosen > 0.0, hidden_ref[r], 0.0)
        valid = wide(valid_ref[low + i], width) > 0.0
        out_ref[...] = jnp.where(valid, total, 0.0).astype(jnp.bfloat16)


def home_kernel(home_ref, *refs):
    blocks, out_ref = refs[:-1], refs[-1]
    rows, width = blocks[0].shape
    for d in range(out_ref.shape[0]):
        total = jnp.zeros((rows, width), jnp.float32)
        for k, block in enumerate(blocks[::-1]):
            chosen = jnp.concatenate([wide(home_ref[d, k], width)] * (rows // 8), 0)
            total = total + jnp.where(chosen > 0.0, block[...].astype(jnp.float32), 0.0)
        out_ref[d] = total.astype(jnp.bfloat16)


def local(
    queries,
    documents,
    doc_len,
    route,
    pair_list,
    attn_gain,
    w_query,
    w_key,
    w_value,
    w_output,
    ffn_gain,
    w_in,
    w_down,
):
    owners = lax.axis_size("pair")
    slices = lax.axis_size("tensor")
    doc_count, doc_rows, width = documents.shape
    query_count, query_rows, _ = queries.shape
    assert query_count * query_rows == doc_rows
    pairs = pair_list.shape[0]
    slots = min(2 * pairs, owners)
    direct = slots == owners
    down_bits = [1 << i for i in range(slices.bit_length() - 1)]
    up_bits = down_bits[::-1]
    attn_gain, ffn_gain = attn_gain.reshape(1, width), ffn_gain.reshape(1, width)
    weights = (w_query, w_key, w_value)

    meta, early, *arrived = kernel_call(
        functools.partial(start_kernel, slots),
        "start",
        (route, doc_len, pair_list, documents, queries),
        [jax.ShapeDtypeStruct((pairs + 1, max(6, owners)), jnp.int32), bf16(1 + direct, 1, doc_rows, width)]
        + [bf16(doc_rows, width)] * owners,
        scratch=[
            pltpu.SMEM(route.shape, jnp.int32),
            pltpu.SMEM(doc_len.shape, jnp.int32),
            pltpu.SMEM(pair_list.shape, jnp.int32),
            pltpu.VMEM(documents.shape, jnp.bfloat16),
            pltpu.VMEM(queries.shape, jnp.bfloat16),
            pltpu.SemaphoreType.DMA((5,)),
        ],
        hbm=(0, 1, 2, 3, 4),
        out_smem=(0,),
        limit=63,
        flops=WAIT,
    )
    arrived = [arrived[k] if k == 0 else swap(arrived[k], k, "pair") for k in range(owners)[::-1]][::-1]
    if not direct:
        me = lax.axis_index("pair")
        taken = lax.dynamic_slice_in_dim(route, me, 1, 1)[:, 0] >= 0
        source = me ^ jnp.arange(owners, dtype=jnp.int32)
        other = jnp.arange(owners, dtype=jnp.int32)
        slot_of = jnp.sum(jnp.where((other[None, :] < source[:, None]) & taken[None, :], 1, 0), 1)
        is_taken = jnp.sum(jnp.where((other[None, :] == source[:, None]) & taken[None, :], 1, 0), 1)
        place = jnp.where(is_taken > 0, slot_of, -1)
        table = (other[:slots, None] == place[None, :]).astype(jnp.bfloat16)
        packed = jnp.einsum("sk,krd->srd", table, jnp.stack(arrived), preferred_element_type=jnp.float32)
        arrived = [packed[s].astype(jnp.bfloat16) for s in range(slots)]
    def spread(kept):
        return kept, swap(kept, up_bits[-1], "tensor")

    top = up_bits[0]
    early = join(early, swap(early, top, "tensor"))
    late = kernel_call(
        stack_kernel, "stack", arrived[direct:][::-1], [bf16(slots - direct, 1, doc_rows, width)], flops=WAIT
    )[0]
    early = gather_blocks(early, up_bits[1:-1])
    first = project("project_early", 1, *spread(early), attn_gain, weights, ())
    late = gather_blocks(join(late, swap(late, top, "tensor")), up_bits[1:-1])
    late, first = tie(late, first)
    late, late_other = spread(late)
    half_done = project_part("project_kept", late, attn_gain, weights)
    q, k, v = project_part(
        "project_came", late_other, attn_gain, weights, tuple(half_done), tuple(first if direct else first[1:])
    )

    groups = [1] * pairs
    swapped = [len(groups) > 1 and g == len(groups) - 1 for g in range(len(groups))]
    part, rest, mine, roles, valid, homes = attend(
        groups, swapped, up_bits, query_rows, doc_count, owners, meta, q, k, v, w_output, late, early if direct else None
    )
    parts = [part]
    if groups[1:]:
        parts += kernel_call(
            functools.partial(output_kernel, groups[1:], swapped[1:]),
            "output",
            (rest, w_output),
            [bf16(2 * n, *part.shape[1:]) for n in groups[1:]],
            flops=2 * rest.size * width,
            moved=2 * w_output.size,
        )
    hidden, pieces = [], []
    for group, part in enumerate(parts):
        order = down_bits[:1] + (down_bits[:0:-1] if swapped[group] else down_bits[1:])
        for bit in order[:-1]:
            kept, came = halve(part, bit)
            part = kept + came
        came = swap(part, order[-1], "tensor")
        own, ffn = settle(sum(groups[:group]), part, came, mine, ffn_gain)
        hidden.append(own)
        pieces += spread(gather_blocks(ffn, order[1:-1][::-1]))
    units = expand(meta, swapped, pieces[::2], w_in, slots)
    units = expand(meta, swapped, pieces[1::2], w_in, slots, tuple(units))[0]
    hidden = jnp.concatenate(hidden, 0)

    columns = 2
    step = width // columns
    pieces = []
    for c in range(columns):
        part = shrink(c * step, step, units, w_down, slices)
        for bit in down_bits:
            kept, came = halve(part, bit)
            if bit != down_bits[-1]:
                part = kept + came
        pieces += [kept, came]
    blocks = kernel_call(
        functools.partial(finish_kernel, 0, columns),
        "finish",
        (roles, valid, hidden, *pieces),
        [bf16(doc_rows, width)] * slots,
    )
    if not direct:
        packed = jnp.einsum("sk,srd->krd", table, jnp.stack(blocks), preferred_element_type=jnp.float32)
        blocks = [packed[s].astype(jnp.bfloat16) for s in range(owners)]
    blocks = [blocks[k] if k == 0 else swap(blocks[k], k, "pair") for k in range(owners)[::-1]][::-1]
    return kernel_call(home_kernel, "home", (homes, *blocks[::-1]), [bf16(doc_count, doc_rows, width)])[0]


def solution(mesh):
    placed = (
        P("pair", "tensor", None),
        P("pair", "tensor", None),
        P(),
        P(),
        P("pair", None),
        P(),
        P(None, "tensor"),
        P(None, "tensor"),
        P(None, "tensor"),
        P("tensor", None),
        P(),
        P(None, "tensor"),
        P("tensor", None),
    )
    return jax.shard_map(
        local, mesh=mesh, in_specs=placed, out_specs=P("pair", "tensor", None), check_vma=False
    )
```

```python
import functools
import math

import jax
import jax.numpy as jnp
from jax import lax
from jax.experimental import pallas as pl
from jax.experimental.pallas import tpu as pltpu
from jax.sharding import PartitionSpec as P

HEAD = 128
MIB = 1024 * 1024
WAIT = 8 * 10**9


def rms_norm(values, gain):
    spread = jnp.mean(values * values, -1, keepdims=True)
    return values * lax.rsqrt(spread + 1e-06) * gain


def swap(values, bit, axis):
    count = lax.axis_size(axis)
    return lax.ppermute(values, axis, [(i, i ^ bit) for i in range(count)])


def gather_blocks(values, bits):
    for bit in bits:
        values = jnp.concatenate([values, swap(values, bit, "tensor")], 1)
    return values


def halve(values, bit):
    half = values.shape[1] // 2
    return values[:, :half], swap(values[:, half:], bit, "tensor")


def tie(first, second):
    return lax.optimization_barrier((first, second))


def ignoring(kernel, at, count, *refs):
    return kernel(*refs[:at], *refs[at + count :])


def kernel_call(
    kernel, name, operands, out_shape, scratch=(), smem=(), out_smem=(), hbm=(), limit=16, flops=0, moved=0, exps=0, after=()
):
    if after:
        kernel = functools.partial(ignoring, kernel, len(operands), len(after))
    anywhere = [pl.BlockSpec(memory_space=pl.ANY)] * len(after)
    space = lambda yes, far=False: pl.BlockSpec(
        memory_space=pltpu.HBM if far else pltpu.SMEM if yes else pltpu.VMEM
    )
    return pl.pallas_call(
        kernel,
        out_shape=out_shape,
        in_specs=[space(i in smem, i in hbm) for i in range(len(operands))] + anywhere,
        out_specs=[space(i in out_smem) for i in range(len(out_shape))],
        scratch_shapes=list(scratch),
        compiler_params=pltpu.CompilerParams(vmem_limit_bytes=limit * MIB),
        cost_estimate=pl.CostEstimate(flops=flops, bytes_accessed=moved, transcendentals=exps),
        name=name,
    )(*operands, *after)


def bf16(*shape):
    return jax.ShapeDtypeStruct(shape, jnp.bfloat16)


def start_kernel(slots, route_hbm, len_hbm, list_hbm, docs_hbm, queries_hbm, meta_ref, early_ref, *refs):
    route_ref, len_ref, list_ref, docs_ref, queries_ref, sems = refs[-6:]
    send_refs = refs[:-6]
    pieces = (
        (route_hbm, route_ref),
        (docs_hbm, docs_ref),
        (queries_hbm, queries_ref),
        (len_hbm, len_ref),
        (list_hbm, list_ref),
    )
    copies = [pltpu.make_async_copy(a, b, sems.at[i]) for i, (a, b) in enumerate(pieces)]
    for copy in copies:
        copy.start()
    owners = route_ref.shape[0]
    doc_count, doc_rows, width = docs_ref.shape
    me = lax.axis_index("pair")
    copies[0].wait()
    copies[1].wait()
    for k in range(owners):
        picked = docs_ref[jnp.maximum(route_ref[me, me ^ k], 0)]
        send_refs[k][...] = picked
        if k == 0 and slots == owners:
            early_ref[1, 0] = picked
    copies[2].wait()
    asked = queries_ref[...].astype(jnp.float32).reshape(doc_rows, width)
    early_ref[0, 0] = asked.astype(jnp.bfloat16)
    copies[3].wait()
    copies[4].wait()
    for p in range(list_ref.shape[0]):
        meta_ref[p, 0] = list_ref[p, 0]
        for role in range(2):
            source = list_ref[p, 1 + role]
            if slots == owners:
                slot = source ^ me
            else:
                slot = jnp.int32(0)
                for j in range(owners):
                    slot = slot + jnp.where((j < source) & (route_ref[j, me] >= 0), 1, 0)
            meta_ref[p, 1 + role] = slot
            meta_ref[p, 3 + role] = len_ref[source * doc_count + jnp.maximum(route_ref[source, me], 0)]
        meta_ref[p, 5] = lax.axis_index("tensor")
    for k in range(owners):
        meta_ref[list_ref.shape[0], k] = route_ref[me, me ^ k]


def normed(values, gain):
    return rms_norm(values.astype(jnp.float32), gain).astype(jnp.bfloat16)


def stack_kernel(*refs):
    for i, ref in enumerate(refs[-2::-1]):
        refs[-1][i, 0] = ref[...]


def join_kernel(kept_ref, came_ref, out_ref):
    out_ref[:, :1] = kept_ref[...]
    out_ref[:, 1:] = came_ref[...]


def join(kept, came):
    slots, _, rows, width = kept.shape
    return kernel_call(join_kernel, "join", (kept, came), [bf16(slots, 2, rows, width)], flops=WAIT)[0]


def project_kernel(lead, kept_ref, came_ref, gain_ref, wq_ref, wk_ref, wv_ref, *refs):
    old, (q_ref, k_ref, v_ref) = refs[: len(refs) - 3], refs[len(refs) - 3 :]
    slots, half, rows, width = kept_ref.shape
    group = half * rows
    tall = slots * group
    tokens = jnp.concatenate([kept_ref[...].reshape(tall, width), came_ref[...].reshape(tall, width)], 0)
    tokens = normed(tokens, gain_ref[...])
    scale = math.log2(math.e) / math.sqrt(HEAD)
    base_q, base_kv = 0, 0
    if old:
        base_q, base_kv = old[0].shape[0] if len(old) == 3 else 0, old[-1].shape[0]
        for ref, new_ref in zip(old, (q_ref, k_ref, v_ref)[3 - len(old) :]):
            new_ref[: ref.shape[0]] = ref[...]

    def store(ref, values, first, base):
        count = slots - first
        for part in range(2):
            for s in range(count):
                begin = part * count * group + s * group
                ref[base + s, part * half : (part + 1) * half] = (
                    values[begin : begin + group].astype(jnp.bfloat16).reshape(half, rows, values.shape[1])
                )

    if lead == slots:
        q_ref[...] = jnp.zeros_like(q_ref)
    else:
        asking = tokens
        if lead:
            asking = jnp.concatenate([tokens[lead * group : tall], tokens[tall + lead * group :]], 0)
        store(q_ref, jnp.dot(asking, wq_ref[...], preferred_element_type=jnp.float32) * scale, lead, base_q)
    store(k_ref, jnp.dot(tokens, wk_ref[...], preferred_element_type=jnp.float32), 0, base_kv)
    store(v_ref, jnp.dot(tokens, wv_ref[...], preferred_element_type=jnp.float32), 0, base_kv)


def project(name, lead, kept, came, gain, weights, old):
    slots, half, rows, width = kept.shape
    wide = weights[0].shape[1]
    have_q = old[0].shape[0] if len(old) == 3 else 0
    have_kv = old[-1].shape[0] if old else 0
    nq, nkv = max(have_q + slots - lead, 1), have_kv + slots
    shape = lambda n: bf16(n, 2 * half, rows, wide)
    return kernel_call(
        functools.partial(project_kernel, lead),
        name,
        (kept, came, gain, *weights, *old),
        [shape(nq), shape(nkv), shape(nkv)],
        limit=32,
        flops=2 * 2 * half * rows * width * wide * (3 * slots - lead),
        moved=6 * width * wide,
    )


def project_part_kernel(scale, rows_ref, gain_ref, wq_ref, wk_ref, wv_ref, *refs):
    olds, outs = refs[:-3], refs[-3:]
    slots, half, rows, width = rows_ref.shape
    tokens = normed(rows_ref[...].reshape(slots * half * rows, width), gain_ref[...])
    kept, ahead = olds[:3], (None,) * (6 - len(olds)) + olds[3:] if olds else ()
    for i, (w_ref, out_ref) in enumerate(zip((wq_ref, wk_ref, wv_ref), outs)):
        values = jnp.dot(tokens, w_ref[...], preferred_element_type=jnp.float32)
        if i == 0:
            values = values * scale
        values = values.astype(jnp.bfloat16).reshape(slots, half, rows, values.shape[1])
        if not olds:
            out_ref[...] = values
            continue
        base = out_ref.shape[0] - slots
        if base:
            out_ref[:base] = ahead[i][...]
        out_ref[base:, :half] = kept[i][...]
        out_ref[base:, half:] = values


def project_part(name, rows_in, gain, weights, kept=(), ahead=()):
    slots, half, rows, width = rows_in.shape
    wide = weights[0].shape[1]
    bases = (0,) * (3 - len(ahead)) + tuple(a.shape[0] for a in ahead)
    return kernel_call(
        functools.partial(project_part_kernel, math.log2(math.e) / math.sqrt(HEAD)),
        name,
        (rows_in, gain, *weights, *kept, *ahead),
        [bf16(base + slots, half * (2 if kept else 1), rows, wide) for base in bases],
        limit=24,
        flops=6 * slots * half * rows * width * wide,
        moved=6 * width * wide,
    )


def attend_kernel(bits, query_rows, owners, others, direct, meta, q_ref, k_ref, v_ref, wo_ref, late_ref, *refs):
    early_ref, refs = (refs[0], refs[1:]) if direct else (None, refs)
    out_ref, rest_ref, mine_ref, role_ref, valid_ref, home_ref, ctx_ref, expo_ref = refs
    _, blocks, rows, width = q_ref.shape
    pairs = meta.shape[0] - 1
    slots = valid_ref.shape[0]
    flag = lambda yes: jnp.full((8, 128), yes.astype(jnp.float32), jnp.float32)
    place = lax.broadcasted_iota(jnp.int32, (rows, 128), 0) + meta[0, 5] * rows
    lengths = [jnp.int32(0)] * slots
    for p in range(pairs):
        for role in range(2):
            slot = meta[p, 1 + role]
            for part, at in enumerate((0, others[p])):
                if direct:
                    chosen = late_ref[jnp.maximum(slot - 1, 0), at]
                    mine_ref[p, role, part] = jnp.where(slot == 0, early_ref[1, at], chosen)
                else:
                    mine_ref[p, role, part] = late_ref[slot, at]
            for s in range(slots):
                role_ref[2 * p + role, s] = flag(slot == s)
                lengths[s] = jnp.where(slot == s, meta[p, 3 + role], lengths[s])
    for s in range(slots):
        valid_ref[s] = (place < lengths[s]).astype(jnp.float32)
    for d in range(home_ref.shape[0]):
        for k in range(owners):
            home_ref[d, k] = flag(meta[pairs, k] == d)
    keys = blocks * rows
    heads = width // HEAD
    lane = lax.broadcasted_iota(jnp.int32, (1, keys), 1)
    block, row = lane // rows, lane % rows
    origin = jnp.zeros_like(lane)
    for place, bit in enumerate(bits):
        origin = origin + ((block >> place) & 1) * bit
    position = (origin ^ meta[0, 5]) * rows + row
    keep = lambda yes: jnp.where(yes, 0.0, jnp.float32(-1e30))
    ones = jnp.ones((3 * keys, HEAD), jnp.bfloat16)

    def rows_of(ref, places, at):
        return jnp.concatenate([ref[place, :, :, at].reshape(keys, HEAD) for place in places], 0)

    def one_pair(pair, carry):
        query, first, second = meta[pair, 0], meta[pair, 1], meta[pair, 2]
        bias = jnp.concatenate(
            [
                keep(position < meta[pair, 3]),
                keep(position < meta[pair, 4]),
                keep((row >= query * query_rows) & (row < (query + 1) * query_rows)),
            ],
            1,
        )
        def weigh(head):
            at = slice(head * HEAD, (head + 1) * HEAD)
            qs = rows_of(q_ref, (first, second), at)
            ks = rows_of(k_ref, (first + 1, second + 1, 0), at)
            scores = lax.dot_general(qs, ks, (((1,), (1,)), ((), ())), preferred_element_type=jnp.float32) + bias
            top = jnp.max(scores, -1, keepdims=True)
            expo_ref[head] = jnp.exp2(scores - top).astype(jnp.bfloat16)

        def mix(head):
            at = slice(head * HEAD, (head + 1) * HEAD)
            vs = rows_of(v_ref, (first + 1, second + 1, 0), at)
            mixed = jnp.dot(expo_ref[head], jnp.concatenate([vs, ones], 1), preferred_element_type=jnp.float32)
            ctx_ref[pl.ds(pl.multiple_of(pair * 2 * keys, 2 * keys), 2 * keys), at] = (
                mixed[:, :HEAD] / mixed[:, HEAD:]
            ).astype(jnp.bfloat16)

        ahead = min(3, heads)
        for head in range(heads + ahead):
            if head < heads:
                weigh(head)
            if head >= ahead:
                mix(head - ahead)
        return carry

    lax.fori_loop(0, pairs, one_pair, 0, unroll=True)
    begin = out_ref.shape[0] * keys
    product = jnp.dot(ctx_ref[:begin], wo_ref[...], preferred_element_type=jnp.float32)
    out_ref[...] = product.astype(jnp.bfloat16).reshape(out_ref.shape)
    if begin < ctx_ref.shape[0]:
        rest_ref[...] = ctx_ref[begin:]


def attend(groups, swapped, bits, query_rows, doc_count, owners, meta, q, k, v, w_output, late, early):
    _, blocks, rows, width = q.shape
    pairs, model, slots, lead = meta.shape[0] - 1, w_output.shape[1], q.shape[0], groups[0]
    others = [late.shape[1] // 2 if far else 1 for n, far in zip(groups, swapped) for _ in range(n)]
    f32 = lambda *shape: jax.ShapeDtypeStruct(shape, jnp.float32)
    tall = 2 * blocks * rows
    return kernel_call(
        functools.partial(attend_kernel, bits, query_rows, owners, others, early is not None),
        "attend",
        (meta, q, k, v, w_output, late) + (() if early is None else (early,)),
        [
            bf16(2 * lead, blocks, rows, model),
            bf16(max(pairs - lead, 1) * tall, width),
            bf16(pairs, 2, 2, *late.shape[2:]),
            f32(2 * pairs, slots, 8, 128),
            f32(slots, rows, 128),
            f32(doc_count, owners, 8, 128),
        ],
        scratch=[
            pltpu.VMEM((pairs * tall, width), jnp.bfloat16),
            pltpu.VMEM((width // HEAD, tall, tall * 3 // 2), jnp.bfloat16),
        ],
        smem=(0,),
        flops=2 * tall * width * (model + 3 * pairs * tall),
        moved=2 * model * width,
        exps=pairs * width // HEAD * tall * tall * 3 // 2,
    )


def turned(blocks):
    bits = blocks.bit_length() - 1
    return [sum(((b >> i) & 1) << (bits - 1 - i) for i in range(bits)) for b in range(blocks)]


def output_kernel(groups, swapped, ctx_ref, wo_ref, *out_refs):
    product = jnp.dot(ctx_ref[...], wo_ref[...], preferred_element_type=jnp.float32).astype(jnp.bfloat16)
    tall = ctx_ref.shape[0] // sum(groups)
    for i, out_ref in enumerate(out_refs):
        begin = sum(groups[:i])
        values = product[begin * tall : (begin + groups[i]) * tall].reshape(out_ref.shape)
        if not swapped[i]:
            out_ref[...] = values
            continue
        half = out_ref.shape[1] // 2
        for b, to in enumerate(turned(half)):
            out_ref[:, to] = values[:, b]
            out_ref[:, half + to] = values[:, half + b]


def settle_kernel(pair, kept_ref, came_ref, mine_ref, gain_ref, hidden_ref, ffn_ref):
    for role in range(kept_ref.shape[0]):
        for part in range(2):
            summed = kept_ref[role, part].astype(jnp.float32) + came_ref[role, 1 - part].astype(jnp.float32)
            hidden = mine_ref[pair + role // 2, role % 2, part].astype(jnp.float32) + summed
            if part == 0:
                hidden_ref[role] = hidden
            ffn_ref[role, part] = rms_norm(hidden, gain_ref[...]).astype(jnp.bfloat16)


def settle(pair, kept, came, mine, gain):
    roles, _, count, width = kept.shape
    return kernel_call(
        functools.partial(settle_kernel, pair),
        "settle",
        (kept, came, mine, gain),
        [jax.ShapeDtypeStruct((roles, count, width), jnp.float32), bf16(roles, 2, count, width)],
    )


def expand_kernel(swapped, tile, meta, w_ref, *refs):
    pieces, rest = refs[: len(swapped)], refs[len(swapped) :]
    old_ref, out_ref = (rest[0] if len(rest) == 2 else None), rest[-1]
    _, half, rows, width = pieces[0].shape
    group = half * rows
    tokens = []
    for piece, far in zip(pieces, swapped):
        for r in range(piece.shape[0]):
            if far:
                tokens += [piece[r, b] for b in turned(half)]
            else:
                tokens.append(piece[r].reshape(group, width))
    tokens = jnp.concatenate(tokens, 0)
    last = out_ref.shape[0] - 1

    def step(i, carry):
        at = pl.ds(pl.multiple_of(i * tile, tile), tile)
        units = jnp.maximum(jnp.dot(tokens, w_ref[:, at], preferred_element_type=jnp.float32), 0.0)
        units = units.astype(jnp.bfloat16)
        if old_ref is not None:
            out_ref[0, :, :, at] = old_ref[0, :, :, at]
        out_ref[last, :, :, at] = jnp.zeros((out_ref.shape[1], group, tile), jnp.bfloat16)
        for r in range(tokens.shape[0] // group):
            slot = meta[r // 2, 1 + r % 2]
            out_ref[last, slot, :, at] = out_ref[last, slot, :, at] + units[r * group : (r + 1) * group]
        return carry

    lax.fori_loop(0, w_ref.shape[1] // tile, step, 0, unroll=4)


def expand(meta, swapped, pieces, w_in, slots, old=()):
    _, half, rows, width = pieces[0].shape
    units = w_in.shape[1]
    roles = sum(piece.shape[0] for piece in pieces)
    return kernel_call(
        functools.partial(expand_kernel, swapped, min(1024, units)),
        "expand",
        (meta, w_in, *pieces, *old),
        [bf16(1 + len(old), slots, half * rows, units)],
        smem=(0,),
        limit=24,
        flops=2 * roles * half * rows * width * units,
        moved=2 * width * units,
    )


def shrink_kernel(begin, units_ref, w_ref, out_ref):
    parts, slots, tall, depth = units_ref.shape
    _, blocks, rows, step = out_ref.shape
    product = jnp.dot(
        units_ref[...].reshape(parts * slots * tall, depth),
        w_ref[:, begin : begin + step],
        preferred_element_type=jnp.float32,
    )
    product = product.astype(jnp.bfloat16).reshape(parts, slots, blocks // parts, rows, step)
    for part in range(parts):
        out_ref[:, part * (blocks // parts) : (part + 1) * (blocks // parts)] = product[part]


def shrink(begin, step, units, w_down, blocks):
    parts, slots, tall, depth = units.shape
    return kernel_call(
        functools.partial(shrink_kernel, begin),
        "shrink",
        (units, w_down),
        [bf16(slots, blocks, parts * tall // blocks, step)],
        limit=24,
        flops=2 * parts * slots * tall * depth * step,
        moved=2 * depth * step,
    )[0]


def wide(flags, width):
    return jnp.concatenate([flags] * (width // 128), 1)


def finish_kernel(low, columns, role_ref, valid_ref, hidden_ref, *refs):
    pieces, out_refs = refs[: 2 * columns], refs[2 * columns :]
    roles, rows, width = hidden_ref.shape
    for i, out_ref in enumerate(out_refs):
        total = jnp.concatenate(
            [
                pieces[2 * c][i, 0].astype(jnp.float32) + pieces[2 * c + 1][i, 0].astype(jnp.float32)
                for c in range(columns)
            ],
            1,
        )
        for r in range(roles):
            chosen = jnp.concatenate([wide(role_ref[r, low + i], width)] * (rows // 8), 0)
            total = total + jnp.where(chosen > 0.0, hidden_ref[r], 0.0)
        valid = wide(valid_ref[low + i], width) > 0.0
        out_ref[...] = jnp.where(valid, total, 0.0).astype(jnp.bfloat16)


def home_kernel(home_ref, *refs):
    blocks, out_ref = refs[:-1], refs[-1]
    rows, width = blocks[0].shape
    for d in range(out_ref.shape[0]):
        total = jnp.zeros((rows, width), jnp.float32)
        for k, block in enumerate(blocks[::-1]):
            chosen = jnp.concatenate([wide(home_ref[d, k], width)] * (rows // 8), 0)
            total = total + jnp.where(chosen > 0.0, block[...].astype(jnp.float32), 0.0)
        out_ref[d] = total.astype(jnp.bfloat16)


def local(
    queries,
    documents,
    doc_len,
    route,
    pair_list,
    attn_gain,
    w_query,
    w_key,
    w_value,
    w_output,
    ffn_gain,
    w_in,
    w_down,
):
    owners = lax.axis_size("pair")
    slices = lax.axis_size("tensor")
    doc_count, doc_rows, width = documents.shape
    query_count, query_rows, _ = queries.shape
    assert query_count * query_rows == doc_rows
    pairs = pair_list.shape[0]
    slots = min(2 * pairs, owners)
    direct = slots == owners
    down_bits = [1 << i for i in range(slices.bit_length() - 1)]
    up_bits = down_bits[::-1]
    attn_gain, ffn_gain = attn_gain.reshape(1, width), ffn_gain.reshape(1, width)
    weights = (w_query, w_key, w_value)

    meta, early, *arrived = kernel_call(
        functools.partial(start_kernel, slots),
        "start",
        (route, doc_len, pair_list, documents, queries),
        [jax.ShapeDtypeStruct((pairs + 1, max(6, owners)), jnp.int32), bf16(1 + direct, 1, doc_rows, width)]
        + [bf16(doc_rows, width)] * owners,
        scratch=[
            pltpu.SMEM(route.shape, jnp.int32),
            pltpu.SMEM(doc_len.shape, jnp.int32),
            pltpu.SMEM(pair_list.shape, jnp.int32),
            pltpu.VMEM(documents.shape, jnp.bfloat16),
            pltpu.VMEM(queries.shape, jnp.bfloat16),
            pltpu.SemaphoreType.DMA((5,)),
        ],
        hbm=(0, 1, 2, 3, 4),
        out_smem=(0,),
        limit=63,
        flops=WAIT,
    )
    arrived = [arrived[k] if k == 0 else swap(arrived[k], k, "pair") for k in range(owners)[::-1]][::-1]
    if not direct:
        me = lax.axis_index("pair")
        taken = lax.dynamic_slice_in_dim(route, me, 1, 1)[:, 0] >= 0
        source = me ^ jnp.arange(owners, dtype=jnp.int32)
        other = jnp.arange(owners, dtype=jnp.int32)
        slot_of = jnp.sum(jnp.where((other[None, :] < source[:, None]) & taken[None, :], 1, 0), 1)
        is_taken = jnp.sum(jnp.where((other[None, :] == source[:, None]) & taken[None, :], 1, 0), 1)
        place = jnp.where(is_taken > 0, slot_of, -1)
        table = (other[:slots, None] == place[None, :]).astype(jnp.bfloat16)
        packed = jnp.einsum("sk,krd->srd", table, jnp.stack(arrived), preferred_element_type=jnp.float32)
        arrived = [packed[s].astype(jnp.bfloat16) for s in range(slots)]
    def spread(kept):
        return kept, swap(kept, up_bits[-1], "tensor")

    top = up_bits[0]
    early = join(early, swap(early, top, "tensor"))
    late = kernel_call(
        stack_kernel, "stack", arrived[direct:][::-1], [bf16(slots - direct, 1, doc_rows, width)], flops=WAIT
    )[0]
    early = gather_blocks(early, up_bits[1:-1])
    first = project("project_early", 1, *spread(early), attn_gain, weights, ())
    late = gather_blocks(join(late, swap(late, top, "tensor")), up_bits[1:-1])
    late, first = tie(late, first)
    late, late_other = spread(late)
    half_done = project_part("project_kept", late, attn_gain, weights)
    q, k, v = project_part(
        "project_came", late_other, attn_gain, weights, tuple(half_done), tuple(first if direct else first[1:])
    )

    groups = [1] * pairs
    swapped = [len(groups) > 1 and g == len(groups) - 1 for g in range(len(groups))]
    part, rest, mine, roles, valid, homes = attend(
        groups, swapped, up_bits, query_rows, doc_count, owners, meta, q, k, v, w_output, late, early if direct else None
    )
    parts = [part]
    if groups[1:]:
        parts += kernel_call(
            functools.partial(output_kernel, groups[1:], swapped[1:]),
            "output",
            (rest, w_output),
            [bf16(2 * n, *part.shape[1:]) for n in groups[1:]],
            flops=2 * rest.size * width,
            moved=2 * w_output.size,
        )
    hidden, pieces = [], []
    for group, part in enumerate(parts):
        order = down_bits[:1] + (down_bits[:0:-1] if swapped[group] else down_bits[1:])
        for bit in order[:-1]:
            kept, came = halve(part, bit)
            part = kept + came
        came = swap(part, order[-1], "tensor")
        own, ffn = settle(sum(groups[:group]), part, came, mine, ffn_gain)
        hidden.append(own)
        pieces += spread(gather_blocks(ffn, order[1:-1][::-1]))
    units = expand(meta, swapped, pieces[::2], w_in, slots)
    units = expand(meta, swapped, pieces[1::2], w_in, slots, tuple(units))[0]
    hidden = jnp.concatenate(hidden, 0)

    columns = 2
    step = width // columns
    pieces = []
    for c in range(columns):
        part = shrink(c * step, step, units, w_down, slices)
        for bit in down_bits:
            kept, came = halve(part, bit)
            if bit != down_bits[-1]:
                part = kept + came
        pieces += [kept, came]
    blocks = kernel_call(
        functools.partial(finish_kernel, 0, columns),
        "finish",
        (roles, valid, hidden, *pieces),
        [bf16(doc_rows, width)] * slots,
    )
    if not direct:
        packed = jnp.einsum("sk,srd->krd", table, jnp.stack(blocks), preferred_element_type=jnp.float32)
        blocks = [packed[s].astype(jnp.bfloat16) for s in range(owners)]
    blocks = [blocks[k] if k == 0 else swap(blocks[k], k, "pair") for k in range(owners)[::-1]][::-1]
    return kernel_call(home_kernel, "home", (homes, *blocks[::-1]), [bf16(doc_count, doc_rows, width)])[0]


def solution(mesh):
    placed = (
        P("pair", "tensor", None),
        P("pair", "tensor", None),
        P(),
        P(),
        P("pair", None),
        P(),
        P(None, "tensor"),
        P(None, "tensor"),
        P(None, "tensor"),
        P("tensor", None),
        P(),
        P(None, "tensor"),
        P("tensor", None),
    )
    return jax.shard_map(
        local, mesh=mesh, in_specs=placed, out_specs=P("pair", "tensor", None), check_vma=False
    )
```
